32 devices in a mesh: gx: 4 (over y, core), gy: 2 (over x), gz: 4 (over z).
Axes of the slice: x: 2, y: 2, z: 4, core: 2. Of those that a mesh axis runs over, the one named last changes fastest.
Arguments:
- stem: bfloat16 [2, 4, 2, 4, 256, 1024], P(None, 'gx', 'gy', 'gz'), may hold values from -6 to 6
- branch_one: bfloat16 [2, 2, 1024, 1024], replicated, may hold values from -0.125 to 0.125
- branch_two: bfloat16 [2, 2, 1024, 1024], P(None, None, ('gy', 'gz')), may hold values from -0.1875 to 0.1875
- branch_three: bfloat16 [2, 2, 1024, 1024], P(None, None, 'gz'), may hold values from -0.125 to 0.125
- slice_values: int32 [3], replicated, may hold values from 0 to 1, as said below
Outputs:
- contracted: bfloat16 [2, 4, 2, 4, 256, 1024], P(None, 'gx', 'gy', 'gz')
The draws below stay inside these ranges and needn't reach their ends.
Inputs may be any that keep to these rules, and one draw needn't show every extreme that they name: `slice_values`: the first two slices differ.
All inputs are finite; a program needn't handle non-finite values.
Results may differ from the reference program's by a relative error of at most 0.0057.
Values may be sent and summed in bfloat16 or wider, within the bound.
A program may use at most 128 MiB of HBM per device.

```python
import jax
import jax.numpy as jnp
from jax import lax

WIDTH = 1024
ROWS = 256
SLICES = 2
N_GX = 4
N_GY = 2
N_GZ = 4


def draw_slice_values(key, part):
    first_key = jax.random.fold_in(key, 11)
    step_key = jax.random.fold_in(key, 12)
    third_key = jax.random.fold_in(key, 13)
    first = jax.random.randint(first_key, (1,), 0, SLICES, dtype=jnp.int32)
    step = jax.random.randint(step_key, (1,), 1, SLICES, dtype=jnp.int32)
    second = (first + step) % SLICES
    third = jax.random.randint(third_key, (1,), 0, SLICES, dtype=jnp.int32)
    return jnp.concatenate([first, second, third]).astype(jnp.int32)


def with_spikes(array, rng, source, target, parts, factor):
    def block_of(dim):
        return (jnp.arange(array.shape[dim]) // (array.shape[dim] // parts)).reshape((-1,) + (1,) * (array.ndim - 1 - dim))

    first = jax.random.permutation(rng, parts)[block_of(target)]
    second = (block_of(target) + parts // 2) % parts
    return jnp.where((block_of(source) == first) | (block_of(source) == second), factor * array, array)


def level_of(stream_key, dims, pieces, low, top_value):
    level, own = 1.0, jax.random.fold_in(stream_key, 6)
    for position, shards_of in pieces:
        steps = jnp.exp(jax.random.uniform(jax.random.fold_in(own, position), (shards_of,), jnp.float32, low / len(pieces), top_value / len(pieces)))
        level = level * jnp.repeat(steps, dims[position] // shards_of).reshape([-1 if axis == position else 1 for axis in range(len(dims))])
    return level


def centred(stream_key, dims, deviation, reach, pieces=(), kind=jnp.bfloat16):
    values = jax.random.normal(stream_key, dims, jnp.float32) * deviation
    if len(pieces) > 0:
        values = level_of(stream_key, dims, pieces, -0.22, 0.18) * values
    return jnp.clip(values, min=-reach, max=reach).astype(kind)


def bell_draw_with(stream_key, extent, width, reach, shards, heavy, kind=jnp.bfloat16):
    values = width * jax.random.normal(stream_key, extent, jnp.float32)
    if shards:
        values = values * level_of(stream_key, extent, shards, -0.22, 0.18)
    return jnp.clip(with_spikes(values, jax.random.fold_in(stream_key, 3), *heavy), -reach, reach).astype(kind)


def setup_inputs(seed: int = 0) -> dict:
    keys = jax.random.split(jax.random.key(seed), 6)
    stem = centred(keys[0], (2, N_GX, N_GY, N_GZ, ROWS, WIDTH), 1.0, 6.0, ((1, 4), (2, 2), (3, 4)))
    branch_one = centred(keys[1], (SLICES, 2, WIDTH, WIDTH), (2 * WIDTH) ** -0.5, 0.125)
    branch_two = bell_draw_with(keys[2], (SLICES, 2, WIDTH, WIDTH), (2 * WIDTH) ** -0.5, 0.1875, ((2, 8),), (2, 3, 8, 2.0))
    branch_three = centred(keys[3], (SLICES, 2, WIDTH, WIDTH), (2 * WIDTH) ** -0.5, 0.125, ((2, 4),))
    slice_values = draw_slice_values(jax.random.fold_in(keys[5], 71), 0)
    return dict(stem=stem, branch_one=branch_one, branch_two=branch_two, branch_three=branch_three, slice_values=slice_values)


def complex_matrix(branch):
    top_half = jnp.concatenate([branch[0], branch[1]], axis=1)
    bottom_half = jnp.concatenate([-branch[1], branch[0]], axis=1)
    return jnp.concatenate([top_half, bottom_half], axis=0)


def complex_product(operand, branch):
    joined = jnp.concatenate([operand[0], operand[1]], axis=1)
    result = jnp.dot(joined, complex_matrix(branch), preferred_element_type=jnp.float32)
    columns = branch.shape[2]
    return jnp.stack([result[:, :columns], result[:, columns:]])


def reference(stem, branch_one, branch_two, branch_three, slice_values):
    group_one = N_GX * N_GY
    group_two = N_GY * N_GZ
    rows_one = ROWS // group_one
    part_one = WIDTH // group_one
    part_two = WIDTH // group_two
    first_branch = lax.dynamic_index_in_dim(branch_one, slice_values[0], 0, keepdims=False)
    second_branch = lax.dynamic_index_in_dim(branch_two, slice_values[1], 0, keepdims=False)
    third_branch = lax.dynamic_index_in_dim(branch_three, slice_values[2], 0, keepdims=False)
    blocks = stem.reshape(2, group_one, N_GZ, N_GX, N_GY, rows_one, part_one, group_one)
    blocks = blocks.transpose(3, 0, 1, 2, 4, 5, 6, 7)

    def one_block(stem_block):
        ordered = stem_block.transpose(0, 3, 2, 4, 6, 1, 5).reshape(2, group_two * ROWS, WIDTH)
        middle = complex_product(ordered, first_branch).astype(jnp.bfloat16)
        middle = middle.reshape(2, group_two, ROWS, part_two, group_two).transpose(0, 2, 4, 1, 3)
        middle = middle.reshape(2, ROWS * group_two, WIDTH)
        second = complex_product(middle, second_branch).astype(jnp.bfloat16)
        second = second.reshape(2, ROWS, group_two, group_two, part_two).transpose(0, 3, 1, 2, 4)
        second = second.reshape(2, group_two * ROWS, WIDTH)
        return complex_product(second, third_branch).astype(jnp.bfloat16)

    mapped = lax.map(one_block, blocks)
    return mapped.transpose(1, 0, 2, 3).reshape(2, N_GX, N_GY, N_GZ, ROWS, WIDTH)
```

```python
import functools

import jax
import jax.numpy as jnp
from jax import lax
from jax.experimental import pallas as pl
from jax.experimental.pallas import tpu as pltpu
from jax.sharding import PartitionSpec as P

WIDTH = 1024
ROWS = 256


def complex_matrix(branch):
    top_half = jnp.concatenate([branch[0], branch[1]], axis=1)
    bottom_half = jnp.concatenate([-branch[1], branch[0]], axis=1)
    return jnp.concatenate([top_half, bottom_half], axis=0)


def complex_product(operand, branch):
    joined = jnp.concatenate([operand[0], operand[1]], axis=1)
    result = jnp.dot(joined, complex_matrix(branch), preferred_element_type=jnp.float32)
    columns = branch.shape[2]
    return jnp.stack([result[:, :columns], result[:, columns:]])


def split_result(result):
    columns = result.shape[1] // 2
    return jnp.stack([result[:, :columns], result[:, columns:]])


def make_accumulate(operand, shard_rows):
    real_part = operand[0]
    imag_part = operand[1]
    joined = jnp.concatenate([real_part, imag_part], axis=1)
    return jnp.dot(joined, complex_matrix(shard_rows), preferred_element_type=jnp.float32)


def third_contraction(operand, branch_three, slice_values):
    local_third = lax.dynamic_index_in_dim(branch_three, slice_values[2], 0, keepdims=False)
    summed = make_accumulate(operand, lax.all_gather(local_third, "gz", axis=1, tiled=True))
    return split_result(summed).astype(jnp.bfloat16)


def body(stem, branch_one, branch_two, branch_three, slice_values):
    count_gx = lax.axis_size("gx")
    count_gy = lax.axis_size("gy")
    count_gz = lax.axis_size("gz")
    group_one = count_gx * count_gy
    group_two = count_gy * count_gz
    rows_one = ROWS // group_one
    rows_two = ROWS // group_two
    part_one = WIDTH // group_one
    part_two = WIDTH // group_two
    first_branch = lax.dynamic_index_in_dim(branch_one, slice_values[0], 0, keepdims=False)
    arrived = lax.all_to_all(
        stem.reshape(2, 1, group_one, rows_one, WIDTH),
        ("gx", "gy"),
        split_axis=2,
        concat_axis=1,
        tiled=True,
    )
    ordered = arrived.reshape(2, group_one, rows_one, part_one, group_one).transpose(0, 2, 4, 1, 3)
    ordered = ordered.reshape(2, ROWS, WIDTH)
    middle = complex_product(ordered, first_branch).astype(jnp.bfloat16)
    gathered = lax.all_to_all(
        middle.reshape(2, group_two, 1, rows_two, WIDTH),
        ("gy", "gz"),
        split_axis=1,
        concat_axis=2,
        tiled=True,
    )
    regrouped = gathered.reshape(2, group_two, rows_two, part_two, group_two).transpose(
        0, 2, 4, 1, 3
    )
    regrouped = regrouped.reshape(2, ROWS, WIDTH)
    local_second = lax.dynamic_index_in_dim(branch_two, slice_values[1], 0, keepdims=False)
    summed = make_accumulate(
        regrouped, lax.all_gather(local_second, ("gy", "gz"), axis=1, tiled=True)
    )
    second = split_result(summed).astype(jnp.bfloat16)
    returned = lax.all_to_all(
        second.reshape(2, 1, rows_two, group_two, group_two, part_two),
        ("gy", "gz"),
        split_axis=4,
        concat_axis=1,
        tiled=True,
    )
    result = third_contraction(returned.reshape(2, ROWS, WIDTH), branch_three, slice_values)
    return result.reshape(stem.shape)


MESH = pl.DeviceIdType.MESH
VMEM_LIMIT = 56 * 1024 * 1024
TILE = 256
LANE = 128


def complex_tile(lhs, rhs):
    result = jnp.dot(lhs, rhs, preferred_element_type=jnp.float32)
    m, n = result.shape[0] // 2, result.shape[1] // 2
    real = result[:m, :n] - result[m:, n:]
    imag = result[m:, :n] + result[:m, n:]
    return real.astype(jnp.bfloat16), imag.astype(jnp.bfloat16)


TILES = WIDTH // TILE


def kernel(
    dims, slices, stem, one_hbm, two_in, three_in, out,
    perm, one, one_perm, two, three, sorted_stem, first, second, third, result,
    local_sem, z_recv, two_recv, three_recv, bulk_recv, sent,
):
    nx, ny, nz = dims
    group = ny * nz
    devices = nx * group
    gx, gy, gz = lax.axis_index("gx"), lax.axis_index("gy"), lax.axis_index("gz")
    line, core = gx // 2, gx % 2
    me = (gx * ny + gy) * nz + gz
    place = gy * nz + gz

    load_one = pltpu.make_async_copy(one_hbm, one, local_sem.at[0])
    load_one.start()

    def coordinates(index):
        return (index // group, (index // nz) % ny, index % nz)

    barrier = pltpu.get_barrier_semaphore()

    def greet(step, carry):
        pl.semaphore_signal(
            barrier, inc=1, device_id=coordinates((me + step) % devices), device_id_type=MESH
        )
        return carry

    lax.fori_loop(1, devices, greet, 0)

    rows_two, rows_three = WIDTH // group, WIDTH // nz
    piece = rows_two // nx
    two[:, pl.ds(pl.multiple_of(place * rows_two, rows_two), rows_two), :] = two_in[slices[1]]
    own_rows = pl.ds(pl.multiple_of(gz * rows_three, rows_three), rows_three)
    for tile in range(TILES):
        three[tile, :, own_rows, :] = three_in[slices[2], :, :, tile * TILE : (tile + 1) * TILE]

    def make_perm(tile, carry):
        column = lax.broadcasted_iota(jnp.int32, (WIDTH, TILE), 1) + tile * TILE
        row = lax.broadcasted_iota(jnp.int32, (WIDTH, TILE), 0)
        wanted = (column % LANE) * group + column // LANE
        perm[tile] = jnp.where(row == wanted, 1.0, 0.0).astype(jnp.bfloat16)
        return carry

    lax.fori_loop(0, TILES, make_perm, 0)
    rows_one = ROWS // nx

    def sort_stem(tile, carry):
        operand = stem[...].reshape(2 * ROWS, WIDTH)
        moved = jnp.dot(operand, perm[tile], preferred_element_type=jnp.float32)
        moved = moved.astype(jnp.bfloat16).reshape(2, nx, rows_one, TILE)
        for x in range(nx):
            for half in range(2):
                sorted_stem[x * group + 2 * tile + half] = moved[
                    :, x, :, half * LANE : (half + 1) * LANE
                ]
        return carry

    lax.fori_loop(0, TILES, sort_stem, 0)
    pl.semaphore_wait(barrier, devices - 1)

    upper = gz // 2
    depth = gz + upper * (nz - 1 - 2 * gz)

    def mirrored(position):
        return position + upper * (nz - 1 - 2 * position)

    def z_of(back):
        return gz if back == 0 else mirrored(1 - depth if back == 1 else back)

    def piece_of(kind, line_of, x, back):
        if kind == 0:
            start = (x * nz + z_of(back)) * rows_two + (line_of * 2 + core) * piece
            return two.at[:, pl.ds(pl.multiple_of(start, piece), piece), :]
        start = z_of(back) * rows_three + ((line_of * 2 + core) * ny + x) * piece
        return three.at[kind - 1, :, pl.ds(pl.multiple_of(start, piece), piece), :]

    other_line, other_x = 1 - line, 1 - gy
    to_line = (other_line * 2 + core, gy, gz)
    to_x = (gx, other_x, gz)
    to_core = (line * 2 + 1 - core, gy, gz)
    BY_XY, BY_CORE, BY_Z, BY_STEM, BY_BACK = range(5)

    def remote(ref, route, arrival, device):
        return pltpu.make_async_remote_copy(
            src_ref=ref, dst_ref=ref, send_sem=sent.at[route], recv_sem=arrival,
            device_id=device, device_id_type=MESH,
        )

    def await_all(ref, route, arrival):
        remote(ref, route, arrival, to_core).wait_recv()

    total = {BY_XY: 0, BY_CORE: 0}

    def send(kind, line_of, x, back, route, arrival, device):
        total[route] += piece if kind == 0 else piece // TILES
        remote(piece_of(kind, line_of, x, back), route, arrival, device).start()

    def rows_of(kind, count):
        if kind == 0:
            return two.at[:, pl.ds(0, count * piece), :]
        return three.at[kind - 1, :, pl.ds(0, count * piece), :]

    def z_copy(kind, back, position):
        return remote(
            piece_of(kind, line, gy, back), BY_Z, z_recv.at[kind, z_of(back)],
            (gx, gy, mirrored(position)),
        )

    def z_start(kind):
        z_copy(kind, 0, 1 - depth).start()

        @pl.when(depth == 1)
        def _():
            z_copy(kind, 0, 2).start()

    def z_pass(kind, back):
        z_copy(kind, back, 0).wait_recv()

        @pl.when(depth == 1)
        def _():
            z_copy(kind, back, 2 if back < 2 else 0).start()

    def arrival_of(kind, name):
        if kind == 0:
            return two_recv.at[name]
        return three_recv.at[kind - 1, name]

    VIA_LINE, VIA_X, VIA_BOTH, VIA_CORE, STEP_X = range(5)

    def to_other_core(kind, line_of, x, back):
        send(kind, line_of, x, back, BY_CORE, arrival_of(kind, VIA_CORE), to_core)

    def two_from_z(step):
        if step > 0:
            z_pass(0, step)
        send(0, line, gy, step, BY_XY, arrival_of(0, STEP_X + step), to_x)
        if step > 0:
            send(0, line, gy, step, BY_XY, arrival_of(0, VIA_LINE), to_line)
            to_other_core(0, line, gy, step)

    def two_from_x(step):
        remote(rows_of(0, 1), BY_XY, arrival_of(0, STEP_X + step), to_x).wait_recv()
        send(0, line, other_x, step, BY_XY, arrival_of(0, VIA_BOTH), to_line)
        to_other_core(0, line, other_x, step)

    def two_from_line():
        await_all(rows_of(0, nz - 1), BY_XY, arrival_of(0, VIA_LINE))
        for step in range(1, nz):
            to_other_core(0, other_line, gy, step)

    def two_from_both():
        await_all(rows_of(0, nz), BY_XY, arrival_of(0, VIA_BOTH))
        for step in range(nz):
            to_other_core(0, other_line, other_x, step)

    def three_from_z(kind):
        for step in range(1, nz):
            z_pass(kind, step)
            send(kind, line, gy, step, BY_XY, arrival_of(kind, VIA_LINE), to_line)
            send(kind, line, gy, step, BY_XY, arrival_of(kind, VIA_X), to_x)
            to_other_core(kind, line, gy, step)

    def three_from_line(kind):
        await_all(rows_of(kind, nz - 1), BY_XY, arrival_of(kind, VIA_LINE))
        for step in range(1, nz):
            send(kind, other_line, gy, step, BY_XY, arrival_of(kind, VIA_BOTH), to_x)
            to_other_core(kind, other_line, gy, step)

    def three_from_x(kind):
        await_all(rows_of(kind, nz - 1), BY_XY, arrival_of(kind, VIA_X))
        for step in range(1, nz):
            to_other_core(kind, line, other_x, step)
        await_all(rows_of(kind, nz - 1), BY_XY, arrival_of(kind, VIA_BOTH))
        for step in range(1, nz):
            to_other_core(kind, other_line, other_x, step)

    def landing(index):
        return first.at[index // nz, :, index % nz]

    def stem_copy(step):
        target = (me + step) % devices
        return pltpu.make_async_remote_copy(
            src_ref=sorted_stem.at[target], dst_ref=landing(me),
            send_sem=sent.at[BY_STEM], recv_sem=bulk_recv.at[0],
            device_id=coordinates(target), device_id_type=MESH,
        )

    def send_stem(step, carry):
        stem_copy(step).start()
        return carry

    def sort_one(tile, carry):
        for part in range(2):
            moved = jnp.dot(
                one[slices[0], part], perm[tile], preferred_element_type=jnp.float32
            ).astype(jnp.bfloat16)
            for half in range(2):
                one_perm[2 * tile + half, :, part * LANE : (part + 1) * LANE] = moved[
                    :, half * LANE : (half + 1) * LANE
                ]
        return carry

    chunk = ROWS // group

    def contract_first(k, carry):
        operand = jnp.concatenate(
            [first[i].reshape(2 * ROWS, LANE) for i in range(group)], axis=1
        )
        for part, value in enumerate(complex_tile(operand, one_perm[k])):
            for c in range(nz):
                for ry in range(ny):
                    row, column = (c * ny + ry) * chunk, (ry * nz + c) * LANE
                    second[part, k, :, column : column + LANE] = value[row : row + chunk]
        return carry

    def contract_second(s, carry):
        operand = second[...].reshape(2 * ROWS, WIDTH)
        columns = pl.ds(pl.multiple_of(s * LANE, LANE), LANE)
        branch = jnp.concatenate([two[0, :, columns], two[1, :, columns]], axis=1)
        for part, value in enumerate(complex_tile(operand, branch)):
            for k in range(group):
                third[part, s, :, k * LANE : (k + 1) * LANE] = value[k * chunk : (k + 1) * chunk]
        return carry

    def back_copy(tile, step):
        target = (place + step) % group
        columns = pl.ds(tile * TILE, TILE)
        return pltpu.make_async_remote_copy(
            src_ref=result.at[target, :, :, columns], dst_ref=out.at[place, :, :, columns],
            send_sem=sent.at[BY_BACK], recv_sem=bulk_recv.at[1],
            device_id=(gx, target // nz, target % nz), device_id_type=MESH,
        )

    def contract_third(tile):
        await_all(rows_of(tile + 1, 4 * (nz - 1)), BY_CORE, arrival_of(tile + 1, VIA_CORE))
        operand = third[...].reshape(2 * ROWS, WIDTH)
        branch = jnp.concatenate([three[tile, 0], three[tile, 1]], axis=1)
        for part, value in enumerate(complex_tile(operand, branch)):
            result[:, part, :, tile * TILE : (tile + 1) * TILE] = value.reshape(group, chunk, TILE)

        def send_back(step, inner):
            back_copy(tile, step).start()
            return inner

        lax.fori_loop(1, group, send_back, 0)

    z_start(0)
    two_from_z(0)
    lax.fori_loop(1, devices, send_stem, 0)
    own = pltpu.make_async_copy(sorted_stem.at[me], landing(me), local_sem.at[1])
    own.start()
    for kind in range(1, TILES + 1):
        z_start(kind)
    load_one.wait()
    for step in range(1, nz):
        sort_one(step - 1, 0)
        two_from_z(step)
    sort_one(TILES - 1, 0)
    for step in range(nz):
        two_from_x(step)
    three_from_z(1)
    two_from_line()
    three_from_z(2)
    three_from_line(1)
    two_from_both()
    own.wait()
    blocks = sorted_stem.at[pl.ds(0, devices - 1)]
    await_all(blocks, BY_STEM, bulk_recv.at[0])
    lax.fori_loop(0, group, contract_first, 0)
    three_from_x(1)
    three_from_line(2)
    three_from_z(3)
    await_all(rows_of(0, 4 * nz - 2), BY_CORE, arrival_of(0, VIA_CORE))
    lax.fori_loop(0, group, contract_second, 0)
    three_from_z(4)
    three_from_line(3)
    three_from_x(2)
    contract_third(0)
    three_from_line(4)
    three_from_x(3)
    contract_third(1)
    three_from_x(4)
    contract_third(2)
    contract_third(3)
    keep = pltpu.make_async_copy(result.at[place], out.at[place], local_sem.at[1])
    keep.start()
    keep.wait()

    for route in (BY_XY, BY_CORE):
        remote(two.at[:, pl.ds(0, total[route]), :], route, bulk_recv.at[0], to_core).wait_send()

    @pl.when(depth == 0)
    def _():
        remote(rows_of(0, 2), BY_Z, bulk_recv.at[0], to_core).wait_send()

    @pl.when(depth == 1)
    def _():
        remote(rows_of(0, 10), BY_Z, bulk_recv.at[0], to_core).wait_send()

    remote(blocks, BY_STEM, bulk_recv.at[0], to_core).wait_send()
    returned = result.at[pl.ds(0, group - 1)]
    remote(returned, BY_BACK, bulk_recv.at[1], to_core).wait()


def fused_body(dims, stem, branch_one, branch_two, branch_three, slice_values):
    nx, ny, nz = dims
    group = ny * nz
    devices = nx * group
    chunk = ROWS // group
    bf16 = jnp.bfloat16
    vmem = pl.BlockSpec(memory_space=pltpu.VMEM)
    dma = pltpu.SemaphoreType.DMA
    blocks = pl.pallas_call(
        functools.partial(kernel, dims),
        out_shape=jax.ShapeDtypeStruct((group, 2, chunk, WIDTH), bf16),
        in_specs=[
            pl.BlockSpec(memory_space=pltpu.SMEM),
            vmem,
            pl.BlockSpec(memory_space=pl.ANY),
            vmem,
            vmem,
        ],
        out_specs=pl.BlockSpec(memory_space=pl.ANY),
        scratch_shapes=[
            pltpu.VMEM((WIDTH // TILE, WIDTH, TILE), bf16),
            pltpu.VMEM(branch_one.shape, bf16),
            pltpu.VMEM((group, WIDTH, 2 * LANE), bf16),
            pltpu.VMEM((2, WIDTH, WIDTH), bf16),
            pltpu.VMEM((TILES, 2, WIDTH, TILE), bf16),
            pltpu.VMEM((devices, 2, ROWS // nx, LANE), bf16),
            pltpu.VMEM((nx * ny, 2, nz, ROWS // nx, LANE), bf16),
            pltpu.VMEM((2, group, chunk, WIDTH), bf16),
            pltpu.VMEM((2, group, chunk, WIDTH), bf16),
            pltpu.VMEM((group, 2, chunk, WIDTH), bf16),
            dma((2,)),
            dma((1 + TILES, nz)),
            dma((4 + nz,)),
            dma((TILES, 4)),
            dma((2,)),
            dma((5,)),
        ],
        compiler_params=pltpu.CompilerParams(
            collective_id=0, has_side_effects=True, vmem_limit_bytes=VMEM_LIMIT
        ),
        cost_estimate=pl.CostEstimate(
            flops=24 * ROWS * WIDTH * WIDTH, bytes_accessed=16 * WIDTH * WIDTH, transcendentals=0
        ),
    )(slice_values, stem.reshape(2, ROWS, WIDTH), branch_one, branch_two, branch_three)
    return blocks.transpose(1, 2, 0, 3).reshape(stem.shape)


def solution(mesh):
    dims = (mesh.shape["gx"], mesh.shape["gy"], mesh.shape["gz"])
    group_one, group_two = dims[0] * dims[1], dims[1] * dims[2]
    fused = group_one == group_two == WIDTH // LANE and dims == (4, 2, 4)
    return jax.shard_map(
        functools.partial(fused_body, dims) if fused else body,
        mesh=mesh,
        in_specs=(
            P(None, "gx", "gy", "gz", None, None),
            P(),
            P(None, None, ("gy", "gz"), None),
            P(None, None, "gz", None),
            P(),
        ),
        out_specs=P(None, "gx", "gy", "gz", None, None),
        check_vma=False,
    )
```

```python
import functools

import jax
import jax.numpy as jnp
from jax import lax
from jax.experimental import pallas as pl
from jax.experimental.pallas import tpu as pltpu
from jax.sharding import PartitionSpec as P

WIDTH = 1024
ROWS = 256


def complex_matrix(branch):
    top_half = jnp.concatenate([branch[0], branch[1]], axis=1)
    bottom_half = jnp.concatenate([-branch[1], branch[0]], axis=1)
    return jnp.concatenate([top_half, bottom_half], axis=0)


def complex_product(operand, branch):
    joined = jnp.concatenate([operand[0], operand[1]], axis=1)
    result = jnp.dot(joined, complex_matrix(branch), preferred_element_type=jnp.float32)
    columns = branch.shape[2]
    return jnp.stack([result[:, :columns], result[:, columns:]])


def split_result(result):
    columns = result.shape[1] // 2
    return jnp.stack([result[:, :columns], result[:, columns:]])


def make_accumulate(operand, shard_rows):
    real_part = operand[0]
    imag_part = operand[1]
    joined = jnp.concatenate([real_part, imag_part], axis=1)
    return jnp.dot(joined, complex_matrix(shard_rows), preferred_element_type=jnp.float32)


def third_contraction(operand, branch_three, slice_values):
    local_third = lax.dynamic_index_in_dim(branch_three, slice_values[2], 0, keepdims=False)
    summed = make_accumulate(operand, lax.all_gather(local_third, "gz", axis=1, tiled=True))
    return split_result(summed).astype(jnp.bfloat16)


def body(stem, branch_one, branch_two, branch_three, slice_values):
    count_gx = lax.axis_size("gx")
    count_gy = lax.axis_size("gy")
    count_gz = lax.axis_size("gz")
    group_one = count_gx * count_gy
    group_two = count_gy * count_gz
    rows_one = ROWS // group_one
    rows_two = ROWS // group_two
    part_one = WIDTH // group_one
    part_two = WIDTH // group_two
    first_branch = lax.dynamic_index_in_dim(branch_one, slice_values[0], 0, keepdims=False)
    arrived = lax.all_to_all(
        stem.reshape(2, 1, group_one, rows_one, WIDTH),
        ("gx", "gy"),
        split_axis=2,
        concat_axis=1,
        tiled=True,
    )
    ordered = arrived.reshape(2, group_one, rows_one, part_one, group_one).transpose(0, 2, 4, 1, 3)
    ordered = ordered.reshape(2, ROWS, WIDTH)
    middle = complex_product(ordered, first_branch).astype(jnp.bfloat16)
    gathered = lax.all_to_all(
        middle.reshape(2, group_two, 1, rows_two, WIDTH),
        ("gy", "gz"),
        split_axis=1,
        concat_axis=2,
        tiled=True,
    )
    regrouped = gathered.reshape(2, group_two, rows_two, part_two, group_two).transpose(
        0, 2, 4, 1, 3
    )
    regrouped = regrouped.reshape(2, ROWS, WIDTH)
    local_second = lax.dynamic_index_in_dim(branch_two, slice_values[1], 0, keepdims=False)
    summed = make_accumulate(
        regrouped, lax.all_gather(local_second, ("gy", "gz"), axis=1, tiled=True)
    )
    second = split_result(summed).astype(jnp.bfloat16)
    returned = lax.all_to_all(
        second.reshape(2, 1, rows_two, group_two, group_two, part_two),
        ("gy", "gz"),
        split_axis=4,
        concat_axis=1,
        tiled=True,
    )
    result = third_contraction(returned.reshape(2, ROWS, WIDTH), branch_three, slice_values)
    return result.reshape(stem.shape)


MESH = pl.DeviceIdType.MESH
VMEM_LIMIT = 56 * 1024 * 1024
TILE = 256
LANE = 128


def complex_tile(lhs, rhs):
    result = jnp.dot(lhs, rhs, preferred_element_type=jnp.float32)
    m, n = result.shape[0] // 2, result.shape[1] // 2
    real = result[:m, :n] - result[m:, n:]
    imag = result[m:, :n] + result[:m, n:]
    return real.astype(jnp.bfloat16), imag.astype(jnp.bfloat16)


TILES = WIDTH // TILE
GROUPS = 2
TILES_IN = TILES // GROUPS


def kernel(
    dims, slices, stem, one_hbm, two_in, three_in, out,
    perm, one, one_perm, two, three, sorted_stem, staged, first, second, third, result,
    local_sem, z_recv, two_recv, three_recv, bulk_recv, sent,
):
    nx, ny, nz = dims
    group = ny * nz
    devices = nx * group
    gx, gy, gz = lax.axis_index("gx"), lax.axis_index("gy"), lax.axis_index("gz")
    line, core = gx // 2, gx % 2
    me = (gx * ny + gy) * nz + gz
    place = gy * nz + gz

    load_one = pltpu.make_async_copy(one_hbm, one, local_sem.at[0])
    load_one.start()

    def coordinates(index):
        return (index // group, (index // nz) % ny, index % nz)

    barrier = pltpu.get_barrier_semaphore()

    def greet(step, carry):
        pl.semaphore_signal(
            barrier, inc=1, device_id=coordinates((me + step) % devices), device_id_type=MESH
        )
        return carry

    lax.fori_loop(1, devices, greet, 0)

    rows_two, rows_three = WIDTH // group, WIDTH // nz
    piece = rows_two // nx
    two[:, pl.ds(pl.multiple_of(place * rows_two, rows_two), rows_two), :] = two_in[slices[1]]
    own_rows = pl.ds(pl.multiple_of(gz * rows_three, rows_three), rows_three)
    for tile in range(TILES):
        three[tile, :, own_rows, :] = three_in[slices[2], :, :, tile * TILE : (tile + 1) * TILE]

    def make_perm(tile, carry):
        column = lax.broadcasted_iota(jnp.int32, (WIDTH, TILE), 1) + tile * TILE
        row = lax.broadcasted_iota(jnp.int32, (WIDTH, TILE), 0)
        wanted = (column % LANE) * group + column // LANE
        perm[tile] = jnp.where(row == wanted, 1.0, 0.0).astype(jnp.bfloat16)
        return carry

    lax.fori_loop(0, TILES, make_perm, 0)
    rows_one = ROWS // nx

    def sort_stem(tile, carry):
        operand = stem[...].reshape(2 * ROWS, WIDTH)
        moved = jnp.dot(operand, perm[tile], preferred_element_type=jnp.float32)
        moved = moved.astype(jnp.bfloat16).reshape(2, nx, rows_one, TILE)
        for x in range(nx):
            for half in range(2):
                target = 2 * tile + half
                sorted_stem[x * ny + target // nz, target % nz] = moved[
                    :, x, :, half * LANE : (half + 1) * LANE
                ]
        return carry

    lax.fori_loop(0, TILES, sort_stem, 0)
    pl.semaphore_wait(barrier, devices - 1)

    upper = gz // 2
    depth = gz + upper * (nz - 1 - 2 * gz)

    def mirrored(position):
        return position + upper * (nz - 1 - 2 * position)

    def z_of(back):
        return gz if back == 0 else mirrored(1 - depth if back == 1 else back)

    def piece_of(kind, line_of, x, back):
        if kind == 0:
            start = (x * nz + z_of(back)) * rows_two + (line_of * 2 + core) * piece
            return two.at[:, pl.ds(pl.multiple_of(start, piece), piece), :]
        start = z_of(back) * rows_three + ((line_of * 2 + core) * ny + x) * piece
        tiles = pl.ds(0, TILES) if kind < 0 else pl.ds((kind - 1) * TILES_IN, TILES_IN)
        return three.at[tiles, :, pl.ds(pl.multiple_of(start, piece), piece), :]

    other_line, other_x = 1 - line, 1 - gy
    to_line = (other_line * 2 + core, gy, gz)
    to_x = (gx, other_x, gz)
    to_core = (line * 2 + 1 - core, gy, gz)
    BY_XY, BY_CORE, BY_Z, BY_STEM, BY_BACK = range(5)

    def remote(ref, route, arrival, device):
        return pltpu.make_async_remote_copy(
            src_ref=ref, dst_ref=ref, send_sem=sent.at[route], recv_sem=arrival,
            device_id=device, device_id_type=MESH,
        )

    def await_all(ref, route, arrival):
        remote(ref, route, arrival, to_core).wait_recv()

    total = {BY_XY: 0, BY_CORE: 0}

    def send(kind, line_of, x, back, route, arrival, device):
        total[route] += piece if kind == 0 else piece // GROUPS
        remote(piece_of(kind, line_of, x, back), route, arrival, device).start()

    def rows_of(kind, count):
        if kind == 0:
            return two.at[:, pl.ds(0, count * piece), :]
        return three.at[pl.ds((kind - 1) * TILES_IN, TILES_IN), :, pl.ds(0, count * piece), :]

    def z_copy(kind, back, position):
        return remote(
            piece_of(kind, line, gy, back), BY_Z, z_recv.at[1 if kind else 0, z_of(back)],
            (gx, gy, mirrored(position)),
        )

    def z_start(kind):
        z_copy(kind, 0, 1 - depth).start()

        @pl.when(depth == 1)
        def _():
            z_copy(kind, 0, 2).start()

    def z_pass(kind, back):
        z_copy(kind, back, 0).wait_recv()

        @pl.when(depth == 1)
        def _():
            z_copy(kind, back, 2 if back < 2 else 0).start()

    def arrival_of(kind, name):
        if kind == 0:
            return two_recv.at[name]
        return three_recv.at[kind - 1, name]

    VIA_CORE, VIA_LINE, VIA_X, VIA_BOTH = range(4)
    TWO_LINE, TWO_X = VIA_X, VIA_X + nz + 1

    def to_other_core(kind, line_of, x, back):
        send(kind, line_of, x, back, BY_CORE, arrival_of(kind, VIA_CORE), to_core)

    def z_through(kind):
        for step in range(1, nz):
            z_pass(kind, step)

    def two_spread(step):
        send(0, line, gy, step, BY_XY, arrival_of(0, TWO_X + step), to_x)
        if step > 0:
            send(0, line, gy, step, BY_XY, arrival_of(0, TWO_LINE + step), to_line)
            to_other_core(0, line, gy, step)

    def two_from_x(step):
        await_all(rows_of(0, 1), BY_XY, arrival_of(0, TWO_X + step))
        if step < nz // 2:
            send(0, line, other_x, step, BY_XY, arrival_of(0, VIA_LINE), to_line)
        to_other_core(0, line, other_x, step)

    def two_from_line(step):
        await_all(rows_of(0, 1), BY_XY, arrival_of(0, TWO_LINE + step))
        if step >= nz // 2:
            send(0, other_line, gy, step, BY_XY, arrival_of(0, TWO_LINE), to_x)
        to_other_core(0, other_line, gy, step)

    def two_from_both():
        await_all(rows_of(0, nz // 2), BY_XY, arrival_of(0, VIA_LINE))
        for step in range(nz // 2):
            to_other_core(0, other_line, other_x, step)
        await_all(rows_of(0, nz // 2), BY_XY, arrival_of(0, TWO_LINE))
        for step in range(nz // 2, nz):
            to_other_core(0, other_line, other_x, step)

    def three_spread(kind):
        for step in range(1, nz):
            send(kind, line, gy, step, BY_XY, arrival_of(kind, VIA_LINE), to_line)
            send(kind, line, gy, step, BY_XY, arrival_of(kind, VIA_X), to_x)
        for step in range(1, nz):
            to_other_core(kind, line, gy, step)

    def three_turn(kind):
        if kind % 2 == 1:
            await_all(rows_of(kind, nz - 1), BY_XY, arrival_of(kind, VIA_LINE))
            near, far = (other_line, gy), to_x
        else:
            await_all(rows_of(kind, nz - 1), BY_XY, arrival_of(kind, VIA_X))
            near, far = (line, other_x), to_line
        for step in range(1, nz):
            send(kind, *near, step, BY_XY, arrival_of(kind, VIA_BOTH), far)
            to_other_core(kind, *near, step)

    def three_last(kind):
        if kind % 2 == 1:
            await_all(rows_of(kind, nz - 1), BY_XY, arrival_of(kind, VIA_X))
            near = (line, other_x)
        else:
            await_all(rows_of(kind, nz - 1), BY_XY, arrival_of(kind, VIA_LINE))
            near = (other_line, gy)
        for step in range(1, nz):
            to_other_core(kind, *near, step)
        await_all(rows_of(kind, nz - 1), BY_XY, arrival_of(kind, VIA_BOTH))
        for step in range(1, nz):
            to_other_core(kind, other_line, other_x, step)

    spot = gx * ny + gy
    plane = nx * ny

    def stem_in_plane(step, carry):
        target = (spot + step) % plane
        pltpu.make_async_remote_copy(
            src_ref=sorted_stem.at[target], dst_ref=staged.at[spot],
            send_sem=sent.at[BY_STEM], recv_sem=bulk_recv.at[0],
            device_id=(target // ny, target % ny, gz), device_id_type=MESH,
        ).start()
        return carry

    def stem_over_z(hop):
        z = (gz + hop) % nz
        pltpu.make_async_remote_copy(
            src_ref=staged.at[:, z], dst_ref=first.at[:, gz],
            send_sem=sent.at[BY_STEM], recv_sem=bulk_recv.at[2],
            device_id=(gx, gy, z), device_id_type=MESH,
        ).start()

    def block_bytes(count):
        return two.at[:, pl.ds(0, count * 8), :]

    def sort_one(tile, carry):
        for part in range(2):
            moved = jnp.dot(
                one[slices[0], part], perm[tile], preferred_element_type=jnp.float32
            ).astype(jnp.bfloat16)
            for half in range(2):
                one_perm[2 * tile + half, :, part * LANE : (part + 1) * LANE] = moved[
                    :, half * LANE : (half + 1) * LANE
                ]
        return carry

    chunk = ROWS // group

    def contract_first(k, carry):
        operand = jnp.concatenate(
            [first[i].swapaxes(0, 1).reshape(2 * ROWS, LANE) for i in range(plane)], axis=1
        )
        for part, value in enumerate(complex_tile(operand, one_perm[k])):
            for c in range(nz):
                for ry in range(ny):
                    row, column = (c * ny + ry) * chunk, (ry * nz + c) * LANE
                    second[part, k, :, column : column + LANE] = value[row : row + chunk]
        return carry

    def contract_second(pair, carry):
        operand = second[...].reshape(2 * ROWS, WIDTH)
        columns = pl.ds(pl.multiple_of(pair * 2 * LANE, 2 * LANE), 2 * LANE)
        branch = jnp.concatenate([two[0, :, columns], two[1, :, columns]], axis=1)
        for part, value in enumerate(complex_tile(operand, branch)):
            for half in range(2):
                for k in range(group):
                    third[part, 2 * pair + half, :, k * LANE : (k + 1) * LANE] = value[
                        k * chunk : (k + 1) * chunk, half * LANE : (half + 1) * LANE
                    ]
        return carry

    def back_copy(tile, step):
        target = (place + step) % group
        columns = pl.ds(tile * TILE, TILE)
        return pltpu.make_async_remote_copy(
            src_ref=result.at[target, :, :, columns], dst_ref=out.at[place, :, :, columns],
            send_sem=sent.at[BY_BACK], recv_sem=bulk_recv.at[1],
            device_id=(gx, target // nz, target % nz), device_id_type=MESH,
        )

    def contract_third(tile):
        if tile % TILES_IN == 0:
            kind = tile // TILES_IN + 1
            await_all(rows_of(kind, 4 * (nz - 1)), BY_CORE, arrival_of(kind, VIA_CORE))
        operand = third[...].reshape(2 * ROWS, WIDTH)
        branch = jnp.concatenate([three[tile, 0], three[tile, 1]], axis=1)
        for part, value in enumerate(complex_tile(operand, branch)):
            result[:, part, :, tile * TILE : (tile + 1) * TILE] = value.reshape(group, chunk, TILE)

        def send_back(step, inner):
            back_copy(tile, step).start()
            return inner

        lax.fori_loop(1, group, send_back, 0)

    z_start(0)
    two_spread(0)
    z_start(-1)
    own = pltpu.make_async_copy(sorted_stem.at[spot], staged.at[spot], local_sem.at[1])
    own.start()
    load_one.wait()
    z_pass(0, 1)
    lax.fori_loop(1, plane, stem_in_plane, 0)
    two_spread(1)
    z_pass(-1, 1)
    two_from_x(0)
    sort_one(0, 0)
    z_pass(0, 2)
    two_spread(2)
    z_pass(0, 3)
    two_spread(3)
    z_pass(-1, 2)
    two_from_x(1)
    two_from_line(1)
    z_pass(-1, 3)
    own.wait()
    await_all(block_bytes((plane - 1) * nz), BY_STEM, bulk_recv.at[0])
    for hop in (2, 1, 3):
        stem_over_z(hop)
    own = pltpu.make_async_copy(staged.at[:, gz], first.at[:, gz], local_sem.at[1])
    own.start()
    three_spread(1)
    two_from_x(2)
    two_from_line(2)
    two_from_x(3)
    two_from_line(3)
    sort_one(1, 0)
    sort_one(2, 0)
    sort_one(3, 0)
    three_turn(1)
    three_spread(2)
    two_from_both()
    three_last(1)
    own.wait()
    await_all(block_bytes((nz - 1) * plane), BY_STEM, bulk_recv.at[2])
    lax.fori_loop(0, group, contract_first, 0)
    three_turn(2)
    await_all(rows_of(0, 4 * nz - 2), BY_CORE, arrival_of(0, VIA_CORE))
    lax.fori_loop(0, 2, contract_second, 0)
    lax.fori_loop(2, 4, contract_second, 0)
    contract_third(0)
    contract_third(1)
    three_last(2)
    contract_third(2)
    contract_third(3)
    keep = pltpu.make_async_copy(result.at[place], out.at[place], local_sem.at[1])
    keep.start()
    keep.wait()

    for route in (BY_XY, BY_CORE):
        remote(two.at[:, pl.ds(0, total[route]), :], route, bulk_recv.at[0], to_core).wait_send()

    @pl.when(depth == 0)
    def _():
        remote(rows_of(0, 2), BY_Z, bulk_recv.at[0], to_core).wait_send()

    @pl.when(depth == 1)
    def _():
        remote(rows_of(0, 10), BY_Z, bulk_recv.at[0], to_core).wait_send()

    remote(block_bytes((plane - 1) * nz + (nz - 1) * plane), BY_STEM, bulk_recv.at[0], to_core).wait_send()
    returned = result.at[pl.ds(0, group - 1)]
    remote(returned, BY_BACK, bulk_recv.at[1], to_core).wait()


def fused_body(dims, stem, branch_one, branch_two, branch_three, slice_values):
    nx, ny, nz = dims
    group = ny * nz
    devices = nx * group
    chunk = ROWS // group
    bf16 = jnp.bfloat16
    vmem = pl.BlockSpec(memory_space=pltpu.VMEM)
    dma = pltpu.SemaphoreType.DMA
    blocks = pl.pallas_call(
        functools.partial(kernel, dims),
        out_shape=jax.ShapeDtypeStruct((group, 2, chunk, WIDTH), bf16),
        in_specs=[
            pl.BlockSpec(memory_space=pltpu.SMEM),
            vmem,
            pl.BlockSpec(memory_space=pl.ANY),
            vmem,
            vmem,
        ],
        out_specs=pl.BlockSpec(memory_space=pl.ANY),
        scratch_shapes=[
            pltpu.VMEM((WIDTH // TILE, WIDTH, TILE), bf16),
            pltpu.VMEM(branch_one.shape, bf16),
            pltpu.VMEM((group, WIDTH, 2 * LANE), bf16),
            pltpu.VMEM((2, WIDTH, WIDTH), bf16),
            pltpu.VMEM((TILES, 2, WIDTH, TILE), bf16),
            pltpu.VMEM((nx * ny, nz, 2, ROWS // nx, LANE), bf16),
            pltpu.VMEM((nx * ny, nz, 2, ROWS // nx, LANE), bf16),
            pltpu.VMEM((nx * ny, nz, 2, ROWS // nx, LANE), bf16),
            pltpu.VMEM((2, group, chunk, WIDTH), bf16),
            pltpu.VMEM((2, group, chunk, WIDTH), bf16),
            pltpu.VMEM((group, 2, chunk, WIDTH), bf16),
            dma((2,)),
            dma((2, nz)),
            dma((3 + 2 * nz,)),
            dma((GROUPS, 4)),
            dma((3,)),
            dma((5,)),
        ],
        compiler_params=pltpu.CompilerParams(
            collective_id=0, has_side_effects=True, vmem_limit_bytes=VMEM_LIMIT
        ),
        cost_estimate=pl.CostEstimate(
            flops=24 * ROWS * WIDTH * WIDTH, bytes_accessed=16 * WIDTH * WIDTH, transcendentals=0
        ),
    )(slice_values, stem.reshape(2, ROWS, WIDTH), branch_one, branch_two, branch_three)
    return blocks.transpose(1, 2, 0, 3).reshape(stem.shape)


def solution(mesh):
    dims = (mesh.shape["gx"], mesh.shape["gy"], mesh.shape["gz"])
    group_one, group_two = dims[0] * dims[1], dims[1] * dims[2]
    fused = group_one == group_two == WIDTH // LANE and dims == (4, 2, 4)
    return jax.shard_map(
        functools.partial(fused_body, dims) if fused else body,
        mesh=mesh,
        in_specs=(
            P(None, "gx", "gy", "gz", None, None),
            P(),
            P(None, None, ("gy", "gz"), None),
            P(None, None, "gz", None),
            P(),
        ),
        out_specs=P(None, "gx", "gy", "gz", None, None),
        check_vma=False,
    )
```

```python
import functools

import jax
import jax.numpy as jnp
from jax import lax
from jax.experimental import pallas as pl
from jax.experimental.pallas import tpu as pltpu
from jax.sharding import PartitionSpec as P

WIDTH = 1024
ROWS = 256


def complex_matrix(branch):
    top_half = jnp.concatenate([branch[0], branch[1]], axis=1)
    bottom_half = jnp.concatenate([-branch[1], branch[0]], axis=1)
    return jnp.concatenate([top_half, bottom_half], axis=0)


def complex_product(operand, branch):
    joined = jnp.concatenate([operand[0], operand[1]], axis=1)
    result = jnp.dot(joined, complex_matrix(branch), preferred_element_type=jnp.float32)
    columns = branch.shape[2]
    return jnp.stack([result[:, :columns], result[:, columns:]])


def split_result(result):
    columns = result.shape[1] // 2
    return jnp.stack([result[:, :columns], result[:, columns:]])


def make_accumulate(operand, shard_rows):
    real_part = operand[0]
    imag_part = operand[1]
    joined = jnp.concatenate([real_part, imag_part], axis=1)
    return jnp.dot(joined, complex_matrix(shard_rows), preferred_element_type=jnp.float32)


def third_contraction(operand, branch_three, slice_values):
    local_third = lax.dynamic_index_in_dim(branch_three, slice_values[2], 0, keepdims=False)
    summed = make_accumulate(operand, lax.all_gather(local_third, "gz", axis=1, tiled=True))
    return split_result(summed).astype(jnp.bfloat16)


def body(stem, branch_one, branch_two, branch_three, slice_values):
    count_gx = lax.axis_size("gx")
    count_gy = lax.axis_size("gy")
    count_gz = lax.axis_size("gz")
    group_one = count_gx * count_gy
    group_two = count_gy * count_gz
    rows_one = ROWS // group_one
    rows_two = ROWS // group_two
    part_one = WIDTH // group_one
    part_two = WIDTH // group_two
    first_branch = lax.dynamic_index_in_dim(branch_one, slice_values[0], 0, keepdims=False)
    arrived = lax.all_to_all(
        stem.reshape(2, 1, group_one, rows_one, WIDTH),
        ("gx", "gy"),
        split_axis=2,
        concat_axis=1,
        tiled=True,
    )
    ordered = arrived.reshape(2, group_one, rows_one, part_one, group_one).transpose(0, 2, 4, 1, 3)
    ordered = ordered.reshape(2, ROWS, WIDTH)
    middle = complex_product(ordered, first_branch).astype(jnp.bfloat16)
    gathered = lax.all_to_all(
        middle.reshape(2, group_two, 1, rows_two, WIDTH),
        ("gy", "gz"),
        split_axis=1,
        concat_axis=2,
        tiled=True,
    )
    regrouped = gathered.reshape(2, group_two, rows_two, part_two, group_two).transpose(
        0, 2, 4, 1, 3
    )
    regrouped = regrouped.reshape(2, ROWS, WIDTH)
    local_second = lax.dynamic_index_in_dim(branch_two, slice_values[1], 0, keepdims=False)
    summed = make_accumulate(
        regrouped, lax.all_gather(local_second, ("gy", "gz"), axis=1, tiled=True)
    )
    second = split_result(summed).astype(jnp.bfloat16)
    returned = lax.all_to_all(
        second.reshape(2, 1, rows_two, group_two, group_two, part_two),
        ("gy", "gz"),
        split_axis=4,
        concat_axis=1,
        tiled=True,
    )
    result = third_contraction(returned.reshape(2, ROWS, WIDTH), branch_three, slice_values)
    return result.reshape(stem.shape)


MESH = pl.DeviceIdType.MESH
VMEM_LIMIT = 56 * 1024 * 1024
TILE = 256
LANE = 128


def complex_tile(lhs, rhs):
    result = jnp.dot(lhs, rhs, preferred_element_type=jnp.float32)
    m, n = result.shape[0] // 2, result.shape[1] // 2
    real = result[:m, :n] - result[m:, n:]
    imag = result[m:, :n] + result[:m, n:]
    return real.astype(jnp.bfloat16), imag.astype(jnp.bfloat16)


TILES = WIDTH // TILE
GROUPS = 2
TILES_IN = TILES // GROUPS


def kernel(
    dims, slices, stem, one_hbm, two_in, three_in, out,
    perm, one, one_perm, two, three, sorted_stem, staged, first, second, third, result,
    local_sem, z_recv, two_recv, three_recv, bulk_recv, sent,
):
    nx, ny, nz = dims
    group = ny * nz
    gx, gy, gz = lax.axis_index("gx"), lax.axis_index("gy"), lax.axis_index("gz")
    line, core = gx // 2, gx % 2
    place = gy * nz + gz

    load_one = pltpu.make_async_copy(one_hbm, one, local_sem.at[0])
    load_one.start()

    barrier = pltpu.get_barrier_semaphore()

    upper = gz // 2
    depth = gz + upper * (nz - 1 - 2 * gz)

    def mirrored(position):
        return position + upper * (nz - 1 - 2 * position)

    spot = gx * ny + gy
    plane = nx * ny

    def greet(device):
        pl.semaphore_signal(barrier, inc=1, device_id=device, device_id_type=MESH)

    def greet_plane(step, carry):
        target = (spot + step) % plane
        greet((target // ny, target % ny, gz))
        return carry

    greet((gx, gy, mirrored(1 - depth)))

    @pl.when(depth == 1)
    def _():
        greet((gx, gy, mirrored(2)))

    lax.fori_loop(1, plane, greet_plane, 0)

    rows_two, rows_three = WIDTH // group, WIDTH // nz
    piece = rows_two // nx
    two[:, pl.ds(pl.multiple_of(place * rows_two, rows_two), rows_two), :] = two_in[slices[1]]
    own_rows = pl.ds(pl.multiple_of(gz * rows_three, rows_three), rows_three)
    for tile in range(TILES):
        three[tile, :, own_rows, :] = three_in[slices[2], :, :, tile * TILE : (tile + 1) * TILE]

    def make_perm(tile, carry):
        column = lax.broadcasted_iota(jnp.int32, (WIDTH, TILE), 1) + tile * TILE
        row = lax.broadcasted_iota(jnp.int32, (WIDTH, TILE), 0)
        wanted = (column % LANE) * group + column // LANE
        perm[tile] = jnp.where(row == wanted, 1.0, 0.0).astype(jnp.bfloat16)
        return carry

    lax.fori_loop(0, TILES, make_perm, 0)
    rows_one = ROWS // nx

    def sort_stem(tile, carry):
        operand = stem[...].reshape(2 * ROWS, WIDTH)
        moved = jnp.dot(operand, perm[tile], preferred_element_type=jnp.float32)
        moved = moved.astype(jnp.bfloat16).reshape(2, nx, rows_one, TILE)
        for x in range(nx):
            for half in range(2):
                target = 2 * tile + half
                sorted_stem[x * ny + target // nz, target % nz] = moved[
                    :, x, :, half * LANE : (half + 1) * LANE
                ]
        return carry

    pl.semaphore_wait(barrier, plane + depth)

    def z_of(back):
        return gz if back == 0 else mirrored(1 - depth if back == 1 else back)

    def piece_of(kind, line_of, x, back):
        if kind == 0:
            start = (x * nz + z_of(back)) * rows_two + (line_of * 2 + core) * piece
            return two.at[:, pl.ds(pl.multiple_of(start, piece), piece), :]
        start = z_of(back) * rows_three + ((line_of * 2 + core) * ny + x) * piece
        tiles = pl.ds(0, TILES) if kind < 0 else pl.ds((kind - 1) * TILES_IN, TILES_IN)
        return three.at[tiles, :, pl.ds(pl.multiple_of(start, piece), piece), :]

    other_line, other_x = 1 - line, 1 - gy
    to_line = (other_line * 2 + core, gy, gz)
    to_x = (gx, other_x, gz)
    to_core = (line * 2 + 1 - core, gy, gz)
    BY_XY, BY_CORE, BY_Z, BY_STEM, BY_BACK = range(5)

    def remote(ref, route, arrival, device):
        return pltpu.make_async_remote_copy(
            src_ref=ref, dst_ref=ref, send_sem=sent.at[route], recv_sem=arrival,
            device_id=device, device_id_type=MESH,
        )

    def await_all(ref, route, arrival):
        remote(ref, route, arrival, to_core).wait_recv()

    total = {BY_XY: 0, BY_CORE: 0}

    def send(kind, line_of, x, back, route, arrival, device):
        total[route] += piece if kind == 0 else piece // GROUPS
        remote(piece_of(kind, line_of, x, back), route, arrival, device).start()

    def rows_of(kind, count):
        if kind == 0:
            return two.at[:, pl.ds(0, count * piece), :]
        return three.at[pl.ds((kind - 1) * TILES_IN, TILES_IN), :, pl.ds(0, count * piece), :]

    def z_copy(kind, back, position):
        return remote(
            piece_of(kind, line, gy, back), BY_Z, z_recv.at[1 if kind else 0, z_of(back)],
            (gx, gy, mirrored(position)),
        )

    def z_start(kind):
        z_copy(kind, 0, 1 - depth).start()

        @pl.when(depth == 1)
        def _():
            z_copy(kind, 0, 2).start()

    def z_pass(kind, back):
        z_copy(kind, back, 0).wait_recv()

        @pl.when(depth == 1)
        def _():
            z_copy(kind, back, 2 if back < 2 else 0).start()

    def arrival_of(kind, name):
        if kind == 0:
            return two_recv.at[name]
        return three_recv.at[kind - 1, name]

    VIA_CORE, VIA_LINE, VIA_X, VIA_BOTH = range(4)
    TWO_LINE, TWO_X = VIA_X, VIA_X + nz + 1

    def to_other_core(kind, line_of, x, back):
        send(kind, line_of, x, back, BY_CORE, arrival_of(kind, VIA_CORE), to_core)

    def z_through(kind):
        for step in range(1, nz):
            z_pass(kind, step)

    def two_spread(step):
        send(0, line, gy, step, BY_XY, arrival_of(0, TWO_X + step), to_x)
        if step > 0:
            send(0, line, gy, step, BY_XY, arrival_of(0, TWO_LINE + step), to_line)
            to_other_core(0, line, gy, step)

    def two_from_x(step):
        await_all(rows_of(0, 1), BY_XY, arrival_of(0, TWO_X + step))
        if step < nz // 2:
            send(0, line, other_x, step, BY_XY, arrival_of(0, VIA_LINE), to_line)
        to_other_core(0, line, other_x, step)

    def two_from_line(step):
        await_all(rows_of(0, 1), BY_XY, arrival_of(0, TWO_LINE + step))
        if step >= nz // 2:
            send(0, other_line, gy, step, BY_XY, arrival_of(0, TWO_LINE), to_x)
        to_other_core(0, other_line, gy, step)

    def two_from_both():
        await_all(rows_of(0, nz // 2), BY_XY, arrival_of(0, VIA_LINE))
        for step in range(nz // 2):
            to_other_core(0, other_line, other_x, step)
        await_all(rows_of(0, nz // 2), BY_XY, arrival_of(0, TWO_LINE))
        for step in range(nz // 2, nz):
            to_other_core(0, other_line, other_x, step)

    def three_spread(kind):
        for step in range(1, nz):
            send(kind, line, gy, step, BY_XY, arrival_of(kind, VIA_LINE), to_line)
            send(kind, line, gy, step, BY_XY, arrival_of(kind, VIA_X), to_x)
        for step in range(1, nz):
            to_other_core(kind, line, gy, step)

    def three_turn(kind):
        if kind % 2 == 1:
            await_all(rows_of(kind, nz - 1), BY_XY, arrival_of(kind, VIA_LINE))
            near, far = (other_line, gy), to_x
        else:
            await_all(rows_of(kind, nz - 1), BY_XY, arrival_of(kind, VIA_X))
            near, far = (line, other_x), to_line
        for step in range(1, nz):
            send(kind, *near, step, BY_XY, arrival_of(kind, VIA_BOTH), far)
            to_other_core(kind, *near, step)

    def three_last(kind):
        if kind % 2 == 1:
            await_all(rows_of(kind, nz - 1), BY_XY, arrival_of(kind, VIA_X))
            near = (line, other_x)
        else:
            await_all(rows_of(kind, nz - 1), BY_XY, arrival_of(kind, VIA_LINE))
            near = (other_line, gy)
        for step in range(1, nz):
            to_other_core(kind, *near, step)
        await_all(rows_of(kind, nz - 1), BY_XY, arrival_of(kind, VIA_BOTH))
        for step in range(1, nz):
            to_other_core(kind, other_line, other_x, step)

    def stem_in_plane(step, carry):
        target = (spot + step) % plane
        pltpu.make_async_remote_copy(
            src_ref=sorted_stem.at[target], dst_ref=staged.at[spot],
            send_sem=sent.at[BY_STEM], recv_sem=bulk_recv.at[0],
            device_id=(target // ny, target % ny, gz), device_id_type=MESH,
        ).start()
        return carry

    def stem_over_z(position):
        z = mirrored(position)
        pltpu.make_async_remote_copy(
            src_ref=staged.at[:, z], dst_ref=first.at[:, gz],
            send_sem=sent.at[BY_STEM], recv_sem=bulk_recv.at[2],
            device_id=(gx, gy, z), device_id_type=MESH,
        ).start()

    def block_bytes(count):
        return two.at[:, pl.ds(0, count * 8), :]

    def sort_one(tile, carry):
        for part in range(2):
            moved = jnp.dot(
                one[slices[0], part], perm[tile], preferred_element_type=jnp.float32
            ).astype(jnp.bfloat16)
            for half in range(2):
                one_perm[2 * tile + half, :, part * LANE : (part + 1) * LANE] = moved[
                    :, half * LANE : (half + 1) * LANE
                ]
        return carry

    chunk = ROWS // group

    def contract_first(k, carry):
        operand = jnp.concatenate(
            [first[i].swapaxes(0, 1).reshape(2 * ROWS, LANE) for i in range(plane)], axis=1
        )
        for part, value in enumerate(complex_tile(operand, one_perm[k])):
            for c in range(nz):
                for ry in range(ny):
                    row, column = (c * ny + ry) * chunk, (ry * nz + c) * LANE
                    second[part, k, :, column : column + LANE] = value[row : row + chunk]
        return carry

    def contract_second(pair, carry):
        operand = second[...].reshape(2 * ROWS, WIDTH)
        columns = pl.ds(pl.multiple_of(pair * 2 * LANE, 2 * LANE), 2 * LANE)
        branch = jnp.concatenate([two[0, :, columns], two[1, :, columns]], axis=1)
        for part, value in enumerate(complex_tile(operand, branch)):
            for half in range(2):
                for k in range(group):
                    third[part, 2 * pair + half, :, k * LANE : (k + 1) * LANE] = value[
                        k * chunk : (k + 1) * chunk, half * LANE : (half + 1) * LANE
                    ]
        return carry

    def back_copy(tile, step):
        target = (place + step) % group
        columns = pl.ds(tile * TILE, TILE)
        return pltpu.make_async_remote_copy(
            src_ref=result.at[target, :, :, columns], dst_ref=out.at[place, :, :, columns],
            send_sem=sent.at[BY_BACK], recv_sem=bulk_recv.at[1],
            device_id=(gx, target // nz, target % nz), device_id_type=MESH,
        )

    def contract_third(tile):
        if tile % TILES_IN == 0:
            kind = tile // TILES_IN + 1
            await_all(rows_of(kind, 4 * (nz - 1)), BY_CORE, arrival_of(kind, VIA_CORE))
        operand = third[...].reshape(2 * ROWS, WIDTH)
        branch = jnp.concatenate([three[tile, 0], three[tile, 1]], axis=1)
        for part, value in enumerate(complex_tile(operand, branch)):
            result[:, part, :, tile * TILE : (tile + 1) * TILE] = value.reshape(group, chunk, TILE)

        def send_back(step, inner):
            back_copy(tile, step).start()
            return inner

        lax.fori_loop(1, group, send_back, 0)

    z_start(0)
    two_spread(0)
    z_start(-1)
    lax.fori_loop(0, TILES, sort_stem, 0)
    lax.fori_loop(1, plane, stem_in_plane, 0)
    own = pltpu.make_async_copy(sorted_stem.at[spot], staged.at[spot], local_sem.at[1])
    own.start()
    z_pass(0, 1)
    two_spread(1)
    z_pass(-1, 1)
    two_from_x(0)
    load_one.wait()
    sort_one(0, 0)
    z_pass(0, 2)
    two_spread(2)
    z_pass(0, 3)
    two_spread(3)
    z_pass(-1, 2)
    own.wait()
    await_all(block_bytes((plane - 1) * nz), BY_STEM, bulk_recv.at[0])
    stem_over_z(2)
    two_from_x(1)
    two_from_line(1)
    z_pass(-1, 3)
    stem_over_z(3)
    stem_over_z(1 - depth)
    own = pltpu.make_async_copy(staged.at[:, gz], first.at[:, gz], local_sem.at[1])
    own.start()
    three_spread(1)
    two_from_x(2)
    two_from_line(2)
    two_from_x(3)
    two_from_line(3)
    sort_one(1, 0)
    sort_one(2, 0)
    sort_one(3, 0)
    three_turn(1)
    three_spread(2)
    two_from_both()
    three_last(1)
    own.wait()
    await_all(block_bytes((nz - 1) * plane), BY_STEM, bulk_recv.at[2])
    lax.fori_loop(0, group, contract_first, 0)
    three_turn(2)
    await_all(rows_of(0, 4 * nz - 2), BY_CORE, arrival_of(0, VIA_CORE))
    lax.fori_loop(0, 2, contract_second, 0)
    lax.fori_loop(2, 4, contract_second, 0)
    contract_third(0)
    contract_third(1)
    three_last(2)
    contract_third(2)
    contract_third(3)
    keep = pltpu.make_async_copy(result.at[place], out.at[place], local_sem.at[1])
    keep.start()
    keep.wait()

    for route in (BY_XY, BY_CORE):
        remote(two.at[:, pl.ds(0, total[route]), :], route, bulk_recv.at[0], to_core).wait_send()

    @pl.when(depth == 0)
    def _():
        remote(rows_of(0, 2), BY_Z, bulk_recv.at[0], to_core).wait_send()

    @pl.when(depth == 1)
    def _():
        remote(rows_of(0, 10), BY_Z, bulk_recv.at[0], to_core).wait_send()

    remote(block_bytes((plane - 1) * nz + (nz - 1) * plane), BY_STEM, bulk_recv.at[0], to_core).wait_send()
    returned = result.at[pl.ds(0, group - 1)]
    remote(returned, BY_BACK, bulk_recv.at[1], to_core).wait()


def fused_body(dims, stem, branch_one, branch_two, branch_three, slice_values):
    nx, ny, nz = dims
    group = ny * nz
    devices = nx * group
    chunk = ROWS // group
    bf16 = jnp.bfloat16
    vmem = pl.BlockSpec(memory_space=pltpu.VMEM)
    dma = pltpu.SemaphoreType.DMA
    blocks = pl.pallas_call(
        functools.partial(kernel, dims),
        out_shape=jax.ShapeDtypeStruct((group, 2, chunk, WIDTH), bf16),
        in_specs=[
            pl.BlockSpec(memory_space=pltpu.SMEM),
            vmem,
            pl.BlockSpec(memory_space=pl.ANY),
            vmem,
            vmem,
        ],
        out_specs=pl.BlockSpec(memory_space=pl.ANY),
        scratch_shapes=[
            pltpu.VMEM((WIDTH // TILE, WIDTH, TILE), bf16),
            pltpu.VMEM(branch_one.shape, bf16),
            pltpu.VMEM((group, WIDTH, 2 * LANE), bf16),
            pltpu.VMEM((2, WIDTH, WIDTH), bf16),
            pltpu.VMEM((TILES, 2, WIDTH, TILE), bf16),
            pltpu.VMEM((nx * ny, nz, 2, ROWS // nx, LANE), bf16),
            pltpu.VMEM((nx * ny, nz, 2, ROWS // nx, LANE), bf16),
            pltpu.VMEM((nx * ny, nz, 2, ROWS // nx, LANE), bf16),
            pltpu.VMEM((2, group, chunk, WIDTH), bf16),
            pltpu.VMEM((2, group, chunk, WIDTH), bf16),
            pltpu.VMEM((group, 2, chunk, WIDTH), bf16),
            dma((2,)),
            dma((2, nz)),
            dma((3 + 2 * nz,)),
            dma((GROUPS, 4)),
            dma((3,)),
            dma((5,)),
        ],
        compiler_params=pltpu.CompilerParams(
            collective_id=0, has_side_effects=True, vmem_limit_bytes=VMEM_LIMIT
        ),
        cost_estimate=pl.CostEstimate(
            flops=24 * ROWS * WIDTH * WIDTH, bytes_accessed=16 * WIDTH * WIDTH, transcendentals=0
        ),
    )(slice_values, stem.reshape(2, ROWS, WIDTH), branch_one, branch_two, branch_three)
    return blocks.transpose(1, 2, 0, 3).reshape(stem.shape)


def solution(mesh):
    dims = (mesh.shape["gx"], mesh.shape["gy"], mesh.shape["gz"])
    group_one, group_two = dims[0] * dims[1], dims[1] * dims[2]
    fused = group_one == group_two == WIDTH // LANE and dims == (4, 2, 4)
    return jax.shard_map(
        functools.partial(fused_body, dims) if fused else body,
        mesh=mesh,
        in_specs=(
            P(None, "gx", "gy", "gz", None, None),
            P(),
            P(None, None, ("gy", "gz"), None),
            P(None, None, "gz", None),
            P(),
        ),
        out_specs=P(None, "gx", "gy", "gz", None, None),
        check_vma=False,
    )
```

```python
import functools

import jax
import jax.numpy as jnp
from jax import lax
from jax.experimental import pallas as pl
from jax.experimental.pallas import tpu as pltpu
from jax.sharding import PartitionSpec as P

WIDTH = 1024
ROWS = 256


def complex_matrix(branch):
    top_half = jnp.concatenate([branch[0], branch[1]], axis=1)
    bottom_half = jnp.concatenate([-branch[1], branch[0]], axis=1)
    return jnp.concatenate([top_half, bottom_half], axis=0)


def complex_product(operand, branch):
    joined = jnp.concatenate([operand[0], operand[1]], axis=1)
    result = jnp.dot(joined, complex_matrix(branch), preferred_element_type=jnp.float32)
    columns = branch.shape[2]
    return jnp.stack([result[:, :columns], result[:, columns:]])


def split_result(result):
    columns = result.shape[1] // 2
    return jnp.stack([result[:, :columns], result[:, columns:]])


def make_accumulate(operand, shard_rows):
    real_part = operand[0]
    imag_part = operand[1]
    joined = jnp.concatenate([real_part, imag_part], axis=1)
    return jnp.dot(joined, complex_matrix(shard_rows), preferred_element_type=jnp.float32)


def third_contraction(operand, branch_three, slice_values):
    local_third = lax.dynamic_index_in_dim(branch_three, slice_values[2], 0, keepdims=False)
    summed = make_accumulate(operand, lax.all_gather(local_third, "gz", axis=1, tiled=True))
    return split_result(summed).astype(jnp.bfloat16)


def body(stem, branch_one, branch_two, branch_three, slice_values):
    count_gx = lax.axis_size("gx")
    count_gy = lax.axis_size("gy")
    count_gz = lax.axis_size("gz")
    group_one = count_gx * count_gy
    group_two = count_gy * count_gz
    rows_one = ROWS // group_one
    rows_two = ROWS // group_two
    part_one = WIDTH // group_one
    part_two = WIDTH // group_two
    first_branch = lax.dynamic_index_in_dim(branch_one, slice_values[0], 0, keepdims=False)
    arrived = lax.all_to_all(
        stem.reshape(2, 1, group_one, rows_one, WIDTH),
        ("gx", "gy"),
        split_axis=2,
        concat_axis=1,
        tiled=True,
    )
    ordered = arrived.reshape(2, group_one, rows_one, part_one, group_one).transpose(0, 2, 4, 1, 3)
    ordered = ordered.reshape(2, ROWS, WIDTH)
    middle = complex_product(ordered, first_branch).astype(jnp.bfloat16)
    gathered = lax.all_to_all(
        middle.reshape(2, group_two, 1, rows_two, WIDTH),
        ("gy", "gz"),
        split_axis=1,
        concat_axis=2,
        tiled=True,
    )
    regrouped = gathered.reshape(2, group_two, rows_two, part_two, group_two).transpose(
        0, 2, 4, 1, 3
    )
    regrouped = regrouped.reshape(2, ROWS, WIDTH)
    local_second = lax.dynamic_index_in_dim(branch_two, slice_values[1], 0, keepdims=False)
    summed = make_accumulate(
        regrouped, lax.all_gather(local_second, ("gy", "gz"), axis=1, tiled=True)
    )
    second = split_result(summed).astype(jnp.bfloat16)
    returned = lax.all_to_all(
        second.reshape(2, 1, rows_two, group_two, group_two, part_two),
        ("gy", "gz"),
        split_axis=4,
        concat_axis=1,
        tiled=True,
    )
    result = third_contraction(returned.reshape(2, ROWS, WIDTH), branch_three, slice_values)
    return result.reshape(stem.shape)


MESH = pl.DeviceIdType.MESH
VMEM_LIMIT = 56 * 1024 * 1024
TILE = 256
LANE = 128


def complex_tile(lhs, rhs):
    result = jnp.dot(lhs, rhs, preferred_element_type=jnp.float32)
    m, n = result.shape[0] // 2, result.shape[1] // 2
    real = result[:m, :n] - result[m:, n:]
    imag = result[m:, :n] + result[:m, n:]
    return real.astype(jnp.bfloat16), imag.astype(jnp.bfloat16)


TILES = WIDTH // TILE
GROUPS = 2
TILES_IN = TILES // GROUPS


def kernel(
    dims, slices, stem, one_hbm, two_in, three_in, out,
    perm, one, one_perm, two, three, sorted_stem, staged, first, second, third, result,
    local_sem, z_recv, two_recv, three_recv, bulk_recv, sent,
):
    nx, ny, nz = dims
    group = ny * nz
    gx, gy, gz = lax.axis_index("gx"), lax.axis_index("gy"), lax.axis_index("gz")
    line, core = gx // 2, gx % 2
    place = gy * nz + gz

    load_one = pltpu.make_async_copy(one_hbm, one, local_sem.at[0])
    load_one.start()

    barrier = pltpu.get_barrier_semaphore()

    upper = gz // 2
    depth = gz + upper * (nz - 1 - 2 * gz)

    def mirrored(position):
        return position + upper * (nz - 1 - 2 * position)

    spot = gx * ny + gy
    plane = nx * ny

    def greet(device):
        pl.semaphore_signal(barrier, inc=1, device_id=device, device_id_type=MESH)

    def greet_plane(step, carry):
        target = (spot + step) % plane
        greet((target // ny, target % ny, gz))
        return carry

    greet((gx, gy, mirrored(1 - depth)))

    @pl.when(depth == 1)
    def _():
        greet((gx, gy, mirrored(2)))

    lax.fori_loop(1, plane, greet_plane, 0)

    rows_two, rows_three = WIDTH // group, WIDTH // nz
    piece = rows_two // nx
    two[:, pl.ds(pl.multiple_of(place * rows_two, rows_two), rows_two), :] = two_in[slices[1]]
    own_rows = pl.ds(pl.multiple_of(gz * rows_three, rows_three), rows_three)
    for tile in range(TILES):
        three[tile, :, own_rows, :] = three_in[slices[2], :, :, tile * TILE : (tile + 1) * TILE]

    def make_perm(tile, carry):
        column = lax.broadcasted_iota(jnp.int32, (WIDTH, TILE), 1) + tile * TILE
        row = lax.broadcasted_iota(jnp.int32, (WIDTH, TILE), 0)
        wanted = (column % LANE) * group + column // LANE
        perm[tile] = jnp.where(row == wanted, 1.0, 0.0).astype(jnp.bfloat16)
        return carry

    lax.fori_loop(0, TILES, make_perm, 0)
    rows_one = ROWS // nx

    def sort_stem(tile, carry):
        operand = stem[...].reshape(2 * ROWS, WIDTH)
        moved = jnp.dot(operand, perm[tile], preferred_element_type=jnp.float32)
        moved = moved.astype(jnp.bfloat16).reshape(2, nx, rows_one, TILE)
        for x in range(nx):
            for half in range(2):
                target = 2 * tile + half
                sorted_stem[x * ny + target // nz, target % nz] = moved[
                    :, x, :, half * LANE : (half + 1) * LANE
                ]
        return carry

    pl.semaphore_wait(barrier, plane + depth)

    def z_of(back):
        return gz if back == 0 else mirrored(1 - depth if back == 1 else back)

    def piece_of(kind, line_of, x, back):
        if kind == 0:
            start = (x * nz + z_of(back)) * rows_two + (line_of * 2 + core) * piece
            return two.at[:, pl.ds(pl.multiple_of(start, piece), piece), :]
        start = z_of(back) * rows_three + ((line_of * 2 + core) * ny + x) * piece
        tiles = pl.ds(0, TILES) if kind < 0 else pl.ds((kind - 1) * TILES_IN, TILES_IN)
        return three.at[tiles, :, pl.ds(pl.multiple_of(start, piece), piece), :]

    other_line, other_x = 1 - line, 1 - gy
    to_line = (other_line * 2 + core, gy, gz)
    to_x = (gx, other_x, gz)
    to_core = (line * 2 + 1 - core, gy, gz)
    BY_XY, BY_CORE, BY_Z, BY_STEM, BY_BACK = range(5)

    def remote(ref, route, arrival, device):
        return pltpu.make_async_remote_copy(
            src_ref=ref, dst_ref=ref, send_sem=sent.at[route], recv_sem=arrival,
            device_id=device, device_id_type=MESH,
        )

    def await_all(ref, route, arrival):
        remote(ref, route, arrival, to_core).wait_recv()

    total = {BY_XY: 0, BY_CORE: 0}

    def send(kind, line_of, x, back, route, arrival, device):
        total[route] += piece if kind == 0 else piece // GROUPS
        remote(piece_of(kind, line_of, x, back), route, arrival, device).start()

    def rows_of(kind, count):
        if kind == 0:
            return two.at[:, pl.ds(0, count * piece), :]
        return three.at[pl.ds((kind - 1) * TILES_IN, TILES_IN), :, pl.ds(0, count * piece), :]

    def z_copy(kind, back, position):
        return remote(
            piece_of(kind, line, gy, back), BY_Z, z_recv.at[1 if kind else 0, z_of(back)],
            (gx, gy, mirrored(position)),
        )

    def z_start(kind):
        z_copy(kind, 0, 1 - depth).start()

        @pl.when(depth == 1)
        def _():
            z_copy(kind, 0, 2).start()

    def z_pass(kind, back):
        z_copy(kind, back, 0).wait_recv()

        @pl.when(depth == 1)
        def _():
            z_copy(kind, back, 2 if back < 2 else 0).start()

    def arrival_of(kind, name):
        if kind == 0:
            return two_recv.at[name]
        return three_recv.at[kind - 1, name]

    VIA_CORE, VIA_LINE, VIA_X, VIA_BOTH = range(4)
    TWO_LINE, TWO_X = VIA_X, VIA_X + nz + 1

    def to_other_core(kind, line_of, x, back):
        send(kind, line_of, x, back, BY_CORE, arrival_of(kind, VIA_CORE), to_core)

    def z_through(kind):
        for step in range(1, nz):
            z_pass(kind, step)

    def two_spread(step):
        send(0, line, gy, step, BY_XY, arrival_of(0, TWO_X + step), to_x)
        if step > 0:
            send(0, line, gy, step, BY_XY, arrival_of(0, TWO_LINE + step), to_line)
            to_other_core(0, line, gy, step)

    def two_from_x(step):
        await_all(rows_of(0, 1), BY_XY, arrival_of(0, TWO_X + step))
        if step < nz // 2:
            send(0, line, other_x, step, BY_XY, arrival_of(0, VIA_LINE), to_line)
        to_other_core(0, line, other_x, step)

    def two_from_line(step):
        await_all(rows_of(0, 1), BY_XY, arrival_of(0, TWO_LINE + step))
        if step >= nz // 2:
            send(0, other_line, gy, step, BY_XY, arrival_of(0, TWO_LINE), to_x)
        to_other_core(0, other_line, gy, step)

    def two_from_both():
        await_all(rows_of(0, nz // 2), BY_XY, arrival_of(0, VIA_LINE))
        for step in range(nz // 2):
            to_other_core(0, other_line, other_x, step)
        await_all(rows_of(0, nz // 2), BY_XY, arrival_of(0, TWO_LINE))
        for step in range(nz // 2, nz):
            to_other_core(0, other_line, other_x, step)

    def three_spread(kind):
        for step in range(1, nz):
            send(kind, line, gy, step, BY_XY, arrival_of(kind, VIA_LINE), to_line)
            send(kind, line, gy, step, BY_XY, arrival_of(kind, VIA_X), to_x)
        for step in range(1, nz):
            to_other_core(kind, line, gy, step)

    def three_turn(kind):
        if kind % 2 == 1:
            await_all(rows_of(kind, nz - 1), BY_XY, arrival_of(kind, VIA_LINE))
            near, far = (other_line, gy), to_x
        else:
            await_all(rows_of(kind, nz - 1), BY_XY, arrival_of(kind, VIA_X))
            near, far = (line, other_x), to_line
        for step in range(1, nz):
            send(kind, *near, step, BY_XY, arrival_of(kind, VIA_BOTH), far)
            to_other_core(kind, *near, step)

    def three_last(kind):
        if kind % 2 == 1:
            await_all(rows_of(kind, nz - 1), BY_XY, arrival_of(kind, VIA_X))
            near = (line, other_x)
        else:
            await_all(rows_of(kind, nz - 1), BY_XY, arrival_of(kind, VIA_LINE))
            near = (other_line, gy)
        for step in range(1, nz):
            to_other_core(kind, *near, step)
        await_all(rows_of(kind, nz - 1), BY_XY, arrival_of(kind, VIA_BOTH))
        for step in range(1, nz):
            to_other_core(kind, other_line, other_x, step)

    def stem_in_plane(step, carry):
        target = (spot + step) % plane
        pltpu.make_async_remote_copy(
            src_ref=sorted_stem.at[target], dst_ref=staged.at[spot],
            send_sem=sent.at[BY_STEM], recv_sem=bulk_recv.at[0],
            device_id=(target // ny, target % ny, gz), device_id_type=MESH,
        ).start()
        return carry

    def stem_over_z(position):
        z = mirrored(position)
        pltpu.make_async_remote_copy(
            src_ref=staged.at[:, z], dst_ref=first.at[:, gz],
            send_sem=sent.at[BY_STEM], recv_sem=bulk_recv.at[2],
            device_id=(gx, gy, z), device_id_type=MESH,
        ).start()

    def block_bytes(count):
        return two.at[:, pl.ds(0, count * 8), :]

    def sort_one(tile, carry):
        for part in range(2):
            moved = jnp.dot(
                one[slices[0], part], perm[tile], preferred_element_type=jnp.float32
            ).astype(jnp.bfloat16)
            for half in range(2):
                one_perm[2 * tile + half, :, part * LANE : (part + 1) * LANE] = moved[
                    :, half * LANE : (half + 1) * LANE
                ]
        return carry

    chunk = ROWS // group

    def contract_first(k, carry):
        operand = jnp.concatenate(
            [first[i].swapaxes(0, 1).reshape(2 * ROWS, LANE) for i in range(plane)], axis=1
        )
        for part, value in enumerate(complex_tile(operand, one_perm[k])):
            for c in range(nz):
                for ry in range(ny):
                    row, column = (c * ny + ry) * chunk, (ry * nz + c) * LANE
                    second[part, k, :, column : column + LANE] = value[row : row + chunk]
        return carry

    def contract_second(pair, carry):
        operand = second[...].reshape(2 * ROWS, WIDTH)
        columns = pl.ds(pl.multiple_of(pair * 2 * LANE, 2 * LANE), 2 * LANE)
        branch = jnp.concatenate([two[0, :, columns], two[1, :, columns]], axis=1)
        for part, value in enumerate(complex_tile(operand, branch)):
            for half in range(2):
                for k in range(group):
                    third[part, 2 * pair + half, :, k * LANE : (k + 1) * LANE] = value[
                        k * chunk : (k + 1) * chunk, half * LANE : (half + 1) * LANE
                    ]
        return carry

    def back_copy(tile, step):
        target = (place + step) % group
        columns = pl.ds(tile * TILE, TILE)
        return pltpu.make_async_remote_copy(
            src_ref=result.at[target, :, :, columns], dst_ref=out.at[place, :, :, columns],
            send_sem=sent.at[BY_BACK], recv_sem=bulk_recv.at[1],
            device_id=(gx, target // nz, target % nz), device_id_type=MESH,
        )

    def contract_third(tile):
        if tile % TILES_IN == 0:
            kind = tile // TILES_IN + 1
            await_all(rows_of(kind, 4 * (nz - 1)), BY_CORE, arrival_of(kind, VIA_CORE))
        operand = third[...].reshape(2 * ROWS, WIDTH)
        branch = jnp.concatenate([three[tile, 0], three[tile, 1]], axis=1)
        for part, value in enumerate(complex_tile(operand, branch)):
            result[:, part, :, tile * TILE : (tile + 1) * TILE] = value.reshape(group, chunk, TILE)

        def send_back(step, inner):
            back_copy(tile, step).start()
            return inner

        lax.fori_loop(1, group, send_back, 0)

    z_start(0)
    two_spread(0)
    z_start(-1)
    lax.fori_loop(0, TILES, sort_stem, 0)
    lax.fori_loop(1, plane, stem_in_plane, 0)
    own = pltpu.make_async_copy(sorted_stem.at[spot], staged.at[spot], local_sem.at[1])
    own.start()
    z_pass(0, 1)
    two_spread(1)
    z_pass(-1, 1)
    two_from_x(0)
    load_one.wait()
    sort_one(0, 0)
    z_pass(0, 2)
    two_spread(2)
    own.wait()
    await_all(block_bytes((plane - 1) * nz), BY_STEM, bulk_recv.at[0])
    stem_over_z(2)
    z_pass(0, 3)
    two_spread(3)
    z_pass(-1, 2)
    two_from_x(1)
    two_from_line(1)
    z_pass(-1, 3)
    stem_over_z(1 - depth)
    stem_over_z(3)
    own = pltpu.make_async_copy(staged.at[:, gz], first.at[:, gz], local_sem.at[1])
    own.start()
    three_spread(1)
    two_from_x(2)
    two_from_line(2)
    two_from_x(3)
    two_from_line(3)
    sort_one(1, 0)
    sort_one(2, 0)
    sort_one(3, 0)
    three_turn(1)
    three_spread(2)
    two_from_both()
    own.wait()
    await_all(block_bytes((nz - 1) * plane), BY_STEM, bulk_recv.at[2])
    lax.fori_loop(0, group, contract_first, 0)
    three_last(1)
    await_all(rows_of(0, 4 * nz - 2), BY_CORE, arrival_of(0, VIA_CORE))
    lax.fori_loop(0, 2, contract_second, 0)
    three_turn(2)
    lax.fori_loop(2, 4, contract_second, 0)
    contract_third(0)
    contract_third(1)
    three_last(2)
    contract_third(2)
    contract_third(3)
    keep = pltpu.make_async_copy(result.at[place], out.at[place], local_sem.at[1])
    keep.start()
    keep.wait()

    for route in (BY_XY, BY_CORE):
        remote(two.at[:, pl.ds(0, total[route]), :], route, bulk_recv.at[0], to_core).wait_send()

    @pl.when(depth == 0)
    def _():
        remote(rows_of(0, 2), BY_Z, bulk_recv.at[0], to_core).wait_send()

    @pl.when(depth == 1)
    def _():
        remote(rows_of(0, 10), BY_Z, bulk_recv.at[0], to_core).wait_send()

    remote(block_bytes((plane - 1) * nz + (nz - 1) * plane), BY_STEM, bulk_recv.at[0], to_core).wait_send()
    returned = result.at[pl.ds(0, group - 1)]
    remote(returned, BY_BACK, bulk_recv.at[1], to_core).wait()


def fused_body(dims, stem, branch_one, branch_two, branch_three, slice_values):
    nx, ny, nz = dims
    group = ny * nz
    devices = nx * group
    chunk = ROWS // group
    bf16 = jnp.bfloat16
    vmem = pl.BlockSpec(memory_space=pltpu.VMEM)
    dma = pltpu.SemaphoreType.DMA
    blocks = pl.pallas_call(
        functools.partial(kernel, dims),
        out_shape=jax.ShapeDtypeStruct((group, 2, chunk, WIDTH), bf16),
        in_specs=[
            pl.BlockSpec(memory_space=pltpu.SMEM),
            vmem,
            pl.BlockSpec(memory_space=pl.ANY),
            vmem,
            vmem,
        ],
        out_specs=pl.BlockSpec(memory_space=pl.ANY),
        scratch_shapes=[
            pltpu.VMEM((WIDTH // TILE, WIDTH, TILE), bf16),
            pltpu.VMEM(branch_one.shape, bf16),
            pltpu.VMEM((group, WIDTH, 2 * LANE), bf16),
            pltpu.VMEM((2, WIDTH, WIDTH), bf16),
            pltpu.VMEM((TILES, 2, WIDTH, TILE), bf16),
            pltpu.VMEM((nx * ny, nz, 2, ROWS // nx, LANE), bf16),
            pltpu.VMEM((nx * ny, nz, 2, ROWS // nx, LANE), bf16),
            pltpu.VMEM((nx * ny, nz, 2, ROWS // nx, LANE), bf16),
            pltpu.VMEM((2, group, chunk, WIDTH), bf16),
            pltpu.VMEM((2, group, chunk, WIDTH), bf16),
            pltpu.VMEM((group, 2, chunk, WIDTH), bf16),
            dma((2,)),
            dma((2, nz)),
            dma((3 + 2 * nz,)),
            dma((GROUPS, 4)),
            dma((3,)),
            dma((5,)),
        ],
        compiler_params=pltpu.CompilerParams(
            collective_id=0, has_side_effects=True, vmem_limit_bytes=VMEM_LIMIT
        ),
        cost_estimate=pl.CostEstimate(
            flops=24 * ROWS * WIDTH * WIDTH, bytes_accessed=16 * WIDTH * WIDTH, transcendentals=0
        ),
    )(slice_values, stem.reshape(2, ROWS, WIDTH), branch_one, branch_two, branch_three)
    return blocks.transpose(1, 2, 0, 3).reshape(stem.shape)


def solution(mesh):
    dims = (mesh.shape["gx"], mesh.shape["gy"], mesh.shape["gz"])
    group_one, group_two = dims[0] * dims[1], dims[1] * dims[2]
    fused = group_one == group_two == WIDTH // LANE and dims == (4, 2, 4)
    return jax.shard_map(
        functools.partial(fused_body, dims) if fused else body,
        mesh=mesh,
        in_specs=(
            P(None, "gx", "gy", "gz", None, None),
            P(),
            P(None, None, ("gy", "gz"), None),
            P(None, None, "gz", None),
            P(),
        ),
        out_specs=P(None, "gx", "gy", "gz", None, None),
        check_vma=False,
    )
```

```python
import functools

import jax
import jax.numpy as jnp
from jax import lax
from jax.experimental import pallas as pl
from jax.experimental.pallas import tpu as pltpu
from jax.sharding import PartitionSpec as P

WIDTH = 1024
ROWS = 256


def complex_matrix(branch):
    top_half = jnp.concatenate([branch[0], branch[1]], axis=1)
    bottom_half = jnp.concatenate([-branch[1], branch[0]], axis=1)
    return jnp.concatenate([top_half, bottom_half], axis=0)


def complex_product(operand, branch):
    joined = jnp.concatenate([operand[0], operand[1]], axis=1)
    result = jnp.dot(joined, complex_matrix(branch), preferred_element_type=jnp.float32)
    columns = branch.shape[2]
    return jnp.stack([result[:, :columns], result[:, columns:]])


def split_result(result):
    columns = result.shape[1] // 2
    return jnp.stack([result[:, :columns], result[:, columns:]])


def make_accumulate(operand, shard_rows):
    real_part = operand[0]
    imag_part = operand[1]
    joined = jnp.concatenate([real_part, imag_part], axis=1)
    return jnp.dot(joined, complex_matrix(shard_rows), preferred_element_type=jnp.float32)


def third_contraction(operand, branch_three, slice_values):
    local_third = lax.dynamic_index_in_dim(branch_three, slice_values[2], 0, keepdims=False)
    summed = make_accumulate(operand, lax.all_gather(local_third, "gz", axis=1, tiled=True))
    return split_result(summed).astype(jnp.bfloat16)


def body(stem, branch_one, branch_two, branch_three, slice_values):
    count_gx = lax.axis_size("gx")
    count_gy = lax.axis_size("gy")
    count_gz = lax.axis_size("gz")
    group_one = count_gx * count_gy
    group_two = count_gy * count_gz
    rows_one = ROWS // group_one
    rows_two = ROWS // group_two
    part_one = WIDTH // group_one
    part_two = WIDTH // group_two
    first_branch = lax.dynamic_index_in_dim(branch_one, slice_values[0], 0, keepdims=False)
    arrived = lax.all_to_all(
        stem.reshape(2, 1, group_one, rows_one, WIDTH),
        ("gx", "gy"),
        split_axis=2,
        concat_axis=1,
        tiled=True,
    )
    ordered = arrived.reshape(2, group_one, rows_one, part_one, group_one).transpose(0, 2, 4, 1, 3)
    ordered = ordered.reshape(2, ROWS, WIDTH)
    middle = complex_product(ordered, first_branch).astype(jnp.bfloat16)
    gathered = lax.all_to_all(
        middle.reshape(2, group_two, 1, rows_two, WIDTH),
        ("gy", "gz"),
        split_axis=1,
        concat_axis=2,
        tiled=True,
    )
    regrouped = gathered.reshape(2, group_two, rows_two, part_two, group_two).transpose(
        0, 2, 4, 1, 3
    )
    regrouped = regrouped.reshape(2, ROWS, WIDTH)
    local_second = lax.dynamic_index_in_dim(branch_two, slice_values[1], 0, keepdims=False)
    summed = make_accumulate(
        regrouped, lax.all_gather(local_second, ("gy", "gz"), axis=1, tiled=True)
    )
    second = split_result(summed).astype(jnp.bfloat16)
    returned = lax.all_to_all(
        second.reshape(2, 1, rows_two, group_two, group_two, part_two),
        ("gy", "gz"),
        split_axis=4,
        concat_axis=1,
        tiled=True,
    )
    result = third_contraction(returned.reshape(2, ROWS, WIDTH), branch_three, slice_values)
    return result.reshape(stem.shape)


MESH = pl.DeviceIdType.MESH
VMEM_LIMIT = 56 * 1024 * 1024
TILE = 256
LANE = 128


def complex_tile(lhs, rhs):
    result = jnp.dot(lhs, rhs, preferred_element_type=jnp.float32)
    m, n = result.shape[0] // 2, result.shape[1] // 2
    real = result[:m, :n] - result[m:, n:]
    imag = result[m:, :n] + result[:m, n:]
    return real.astype(jnp.bfloat16), imag.astype(jnp.bfloat16)


TILES = WIDTH // TILE
GROUPS = 2
TILES_IN = TILES // GROUPS


def kernel(
    dims, slices, stem, one_hbm, two_in, three_in, out,
    perm, one, one_perm, two, three, sorted_stem, staged, first, second, third, result,
    local_sem, z_recv, two_recv, three_recv, bulk_recv, sent,
):
    nx, ny, nz = dims
    group = ny * nz
    gx, gy, gz = lax.axis_index("gx"), lax.axis_index("gy"), lax.axis_index("gz")
    line, core = gx // 2, gx % 2
    place = gy * nz + gz

    load_one = pltpu.make_async_copy(one_hbm, one, local_sem.at[0])
    load_one.start()

    barrier = pltpu.get_barrier_semaphore()

    upper = gz // 2
    depth = gz + upper * (nz - 1 - 2 * gz)

    def mirrored(position):
        return position + upper * (nz - 1 - 2 * position)

    spot = gx * ny + gy
    plane = nx * ny

    def greet(device):
        pl.semaphore_signal(barrier, inc=1, device_id=device, device_id_type=MESH)

    def greet_plane(step, carry):
        target = (spot + step) % plane
        greet((target // ny, target % ny, gz))
        return carry

    greet((gx, gy, mirrored(1 - depth)))

    @pl.when(depth == 1)
    def _():
        greet((gx, gy, mirrored(2)))

    lax.fori_loop(1, plane, greet_plane, 0)

    rows_two, rows_three = WIDTH // group, WIDTH // nz
    piece = rows_two // nx
    two[:, pl.ds(pl.multiple_of(place * rows_two, rows_two), rows_two), :] = two_in[slices[1]]
    own_rows = pl.ds(pl.multiple_of(gz * rows_three, rows_three), rows_three)
    for tile in range(TILES):
        three[tile, :, own_rows, :] = three_in[slices[2], :, :, tile * TILE : (tile + 1) * TILE]

    def make_perm(tile, carry):
        column = lax.broadcasted_iota(jnp.int32, (WIDTH, TILE), 1) + tile * TILE
        row = lax.broadcasted_iota(jnp.int32, (WIDTH, TILE), 0)
        wanted = (column % LANE) * group + column // LANE
        perm[tile] = jnp.where(row == wanted, 1.0, 0.0).astype(jnp.bfloat16)
        return carry

    lax.fori_loop(0, TILES, make_perm, 0)
    rows_one = ROWS // nx

    def sort_stem(tile, carry):
        operand = stem[...].reshape(2 * ROWS, WIDTH)
        moved = jnp.dot(operand, perm[tile], preferred_element_type=jnp.float32)
        moved = moved.astype(jnp.bfloat16).reshape(2, nx, rows_one, TILE)
        for x in range(nx):
            for half in range(2):
                target = 2 * tile + half
                sorted_stem[x * ny + target // nz, target % nz] = moved[
                    :, x, :, half * LANE : (half + 1) * LANE
                ]
        return carry

    pl.semaphore_wait(barrier, plane + depth)

    def z_of(back):
        return gz if back == 0 else mirrored(1 - depth if back == 1 else back)

    def piece_of(kind, line_of, x, back):
        if kind == 0:
            start = (x * nz + z_of(back)) * rows_two + (line_of * 2 + core) * piece
            return two.at[:, pl.ds(pl.multiple_of(start, piece), piece), :]
        start = z_of(back) * rows_three + ((line_of * 2 + core) * ny + x) * piece
        tiles = pl.ds(0, TILES) if kind < 0 else pl.ds((kind - 1) * TILES_IN, TILES_IN)
        return three.at[tiles, :, pl.ds(pl.multiple_of(start, piece), piece), :]

    other_line, other_x = 1 - line, 1 - gy
    to_line = (other_line * 2 + core, gy, gz)
    to_x = (gx, other_x, gz)
    to_core = (line * 2 + 1 - core, gy, gz)
    BY_XY, BY_CORE, BY_Z, BY_STEM, BY_BACK = range(5)

    def remote(ref, route, arrival, device):
        return pltpu.make_async_remote_copy(
            src_ref=ref, dst_ref=ref, send_sem=sent.at[route], recv_sem=arrival,
            device_id=device, device_id_type=MESH,
        )

    def await_all(ref, route, arrival):
        remote(ref, route, arrival, to_core).wait_recv()

    total = {BY_XY: 0, BY_CORE: 0}

    def send(kind, line_of, x, back, route, arrival, device):
        total[route] += piece if kind == 0 else piece // GROUPS
        remote(piece_of(kind, line_of, x, back), route, arrival, device).start()

    def rows_of(kind, count):
        if kind == 0:
            return two.at[:, pl.ds(0, count * piece), :]
        return three.at[pl.ds((kind - 1) * TILES_IN, TILES_IN), :, pl.ds(0, count * piece), :]

    def z_copy(kind, back, position):
        return remote(
            piece_of(kind, line, gy, back), BY_Z, z_recv.at[1 if kind else 0, z_of(back)],
            (gx, gy, mirrored(position)),
        )

    def z_start(kind):
        z_copy(kind, 0, 1 - depth).start()

        @pl.when(depth == 1)
        def _():
            z_copy(kind, 0, 2).start()

    def z_pass(kind, back):
        z_copy(kind, back, 0).wait_recv()

        @pl.when(depth == 1)
        def _():
            z_copy(kind, back, 2 if back < 2 else 0).start()

    def arrival_of(kind, name):
        if kind == 0:
            return two_recv.at[name]
        return three_recv.at[kind - 1, name]

    VIA_CORE, VIA_LINE, VIA_X, VIA_BOTH = range(4)
    TWO_LINE, TWO_X = VIA_X, VIA_X + nz + 1

    def to_other_core(kind, line_of, x, back):
        send(kind, line_of, x, back, BY_CORE, arrival_of(kind, VIA_CORE), to_core)

    def z_through(kind):
        for step in range(1, nz):
            z_pass(kind, step)

    def two_spread(step):
        send(0, line, gy, step, BY_XY, arrival_of(0, TWO_X + step), to_x)
        if step > 0:
            send(0, line, gy, step, BY_XY, arrival_of(0, TWO_LINE + step), to_line)
            to_other_core(0, line, gy, step)

    def two_from_x(step):
        await_all(rows_of(0, 1), BY_XY, arrival_of(0, TWO_X + step))
        if step < nz // 2:
            send(0, line, other_x, step, BY_XY, arrival_of(0, VIA_LINE), to_line)
        to_other_core(0, line, other_x, step)

    def two_from_line(step):
        await_all(rows_of(0, 1), BY_XY, arrival_of(0, TWO_LINE + step))
        if step >= nz // 2:
            send(0, other_line, gy, step, BY_XY, arrival_of(0, TWO_LINE), to_x)
        to_other_core(0, other_line, gy, step)

    def two_from_both():
        await_all(rows_of(0, nz // 2), BY_XY, arrival_of(0, VIA_LINE))
        for step in range(nz // 2):
            to_other_core(0, other_line, other_x, step)
        await_all(rows_of(0, nz // 2), BY_XY, arrival_of(0, TWO_LINE))
        for step in range(nz // 2, nz):
            to_other_core(0, other_line, other_x, step)

    def three_spread(kind):
        for step in range(1, nz):
            send(kind, line, gy, step, BY_XY, arrival_of(kind, VIA_LINE), to_line)
            send(kind, line, gy, step, BY_XY, arrival_of(kind, VIA_X), to_x)
        for step in range(1, nz):
            to_other_core(kind, line, gy, step)

    def three_turn(kind):
        if kind % 2 == 1:
            await_all(rows_of(kind, nz - 1), BY_XY, arrival_of(kind, VIA_LINE))
            near, far = (other_line, gy), to_x
        else:
            await_all(rows_of(kind, nz - 1), BY_XY, arrival_of(kind, VIA_X))
            near, far = (line, other_x), to_line
        for step in range(1, nz):
            send(kind, *near, step, BY_XY, arrival_of(kind, VIA_BOTH), far)
            to_other_core(kind, *near, step)

    def three_last(kind):
        if kind % 2 == 1:
            await_all(rows_of(kind, nz - 1), BY_XY, arrival_of(kind, VIA_X))
            near = (line, other_x)
        else:
            await_all(rows_of(kind, nz - 1), BY_XY, arrival_of(kind, VIA_LINE))
            near = (other_line, gy)
        for step in range(1, nz):
            to_other_core(kind, *near, step)
        await_all(rows_of(kind, nz - 1), BY_XY, arrival_of(kind, VIA_BOTH))
        for step in range(1, nz):
            to_other_core(kind, other_line, other_x, step)

    def stem_in_plane(step, carry):
        target = (spot + step) % plane
        pltpu.make_async_remote_copy(
            src_ref=sorted_stem.at[target], dst_ref=staged.at[spot],
            send_sem=sent.at[BY_STEM], recv_sem=bulk_recv.at[0],
            device_id=(target // ny, target % ny, gz), device_id_type=MESH,
        ).start()
        return carry

    def stem_over_z(position):
        z = mirrored(position)
        pltpu.make_async_remote_copy(
            src_ref=staged.at[:, z], dst_ref=first.at[:, gz],
            send_sem=sent.at[BY_STEM], recv_sem=bulk_recv.at[2],
            device_id=(gx, gy, z), device_id_type=MESH,
        ).start()

    def block_bytes(count):
        return two.at[:, pl.ds(0, count * 8), :]

    def sort_one(tile, carry):
        for part in range(2):
            moved = jnp.dot(
                one[slices[0], part], perm[tile], preferred_element_type=jnp.float32
            ).astype(jnp.bfloat16)
            for half in range(2):
                one_perm[2 * tile + half, :, part * LANE : (part + 1) * LANE] = moved[
                    :, half * LANE : (half + 1) * LANE
                ]
        return carry

    chunk = ROWS // group

    def contract_first(k, carry):
        operand = jnp.concatenate(
            [first[i].swapaxes(0, 1).reshape(2 * ROWS, LANE) for i in range(plane)], axis=1
        )
        for part, value in enumerate(complex_tile(operand, one_perm[k])):
            for c in range(nz):
                for ry in range(ny):
                    row, column = (c * ny + ry) * chunk, (ry * nz + c) * LANE
                    second[part, k, :, column : column + LANE] = value[row : row + chunk]
        return carry

    def contract_second(pair, carry):
        operand = second[...].reshape(2 * ROWS, WIDTH)
        columns = pl.ds(pl.multiple_of(pair * 2 * LANE, 2 * LANE), 2 * LANE)
        branch = jnp.concatenate([two[0, :, columns], two[1, :, columns]], axis=1)
        for part, value in enumerate(complex_tile(operand, branch)):
            for half in range(2):
                for k in range(group):
                    third[part, 2 * pair + half, :, k * LANE : (k + 1) * LANE] = value[
                        k * chunk : (k + 1) * chunk, half * LANE : (half + 1) * LANE
                    ]
        return carry

    def back_copy(tile, step):
        target = (place + step) % group
        columns = pl.ds(tile * TILE, TILE)
        return pltpu.make_async_remote_copy(
            src_ref=result.at[target, :, :, columns], dst_ref=out.at[place, :, :, columns],
            send_sem=sent.at[BY_BACK], recv_sem=bulk_recv.at[1],
            device_id=(gx, target // nz, target % nz), device_id_type=MESH,
        )

    def contract_third(tile):
        if tile % TILES_IN == 0:
            kind = tile // TILES_IN + 1
            await_all(rows_of(kind, 4 * (nz - 1)), BY_CORE, arrival_of(kind, VIA_CORE))
        operand = third[...].reshape(2 * ROWS, WIDTH)
        branch = jnp.concatenate([three[tile, 0], three[tile, 1]], axis=1)
        for part, value in enumerate(complex_tile(operand, branch)):
            result[:, part, :, tile * TILE : (tile + 1) * TILE] = value.reshape(group, chunk, TILE)

        def send_back(step, inner):
            back_copy(tile, step).start()
            return inner

        lax.fori_loop(1, group, send_back, 0)

    z_start(0)
    two_spread(0)
    z_start(-1)
    lax.fori_loop(0, TILES, sort_stem, 0)
    lax.fori_loop(1, plane, stem_in_plane, 0)
    own = pltpu.make_async_copy(sorted_stem.at[spot], staged.at[spot], local_sem.at[1])
    own.start()
    z_pass(0, 1)
    two_spread(1)
    z_pass(-1, 1)
    two_from_x(0)
    load_one.wait()
    sort_one(0, 0)
    z_pass(0, 2)
    two_spread(2)
    own.wait()
    await_all(block_bytes((plane - 1) * nz), BY_STEM, bulk_recv.at[0])
    stem_over_z(2)
    z_pass(0, 3)
    two_spread(3)
    z_pass(-1, 2)
    two_from_x(1)
    two_from_line(1)
    z_pass(-1, 3)
    stem_over_z(1 - depth)
    stem_over_z(3)
    own = pltpu.make_async_copy(staged.at[:, gz], first.at[:, gz], local_sem.at[1])
    own.start()
    three_spread(1)
    two_from_x(2)
    two_from_line(2)
    two_from_x(3)
    two_from_line(3)
    sort_one(1, 0)
    sort_one(2, 0)
    sort_one(3, 0)
    three_turn(1)
    three_spread(2)
    two_from_both()
    own.wait()
    await_all(block_bytes((nz - 1) * plane), BY_STEM, bulk_recv.at[2])
    lax.fori_loop(0, group, contract_first, 0)
    three_last(1)
    await_all(rows_of(0, 4 * nz - 2), BY_CORE, arrival_of(0, VIA_CORE))
    lax.fori_loop(0, 2, contract_second, 0)
    lax.fori_loop(2, 4, contract_second, 0)
    three_turn(2)
    contract_third(0)
    contract_third(1)
    three_last(2)
    contract_third(2)
    contract_third(3)
    keep = pltpu.make_async_copy(result.at[place], out.at[place], local_sem.at[1])
    keep.start()
    keep.wait()

    for route in (BY_XY, BY_CORE):
        remote(two.at[:, pl.ds(0, total[route]), :], route, bulk_recv.at[0], to_core).wait_send()

    @pl.when(depth == 0)
    def _():
        remote(rows_of(0, 2), BY_Z, bulk_recv.at[0], to_core).wait_send()

    @pl.when(depth == 1)
    def _():
        remote(rows_of(0, 10), BY_Z, bulk_recv.at[0], to_core).wait_send()

    remote(block_bytes((plane - 1) * nz + (nz - 1) * plane), BY_STEM, bulk_recv.at[0], to_core).wait_send()
    returned = result.at[pl.ds(0, group - 1)]
    remote(returned, BY_BACK, bulk_recv.at[1], to_core).wait()


def fused_body(dims, stem, branch_one, branch_two, branch_three, slice_values):
    nx, ny, nz = dims
    group = ny * nz
    devices = nx * group
    chunk = ROWS // group
    bf16 = jnp.bfloat16
    vmem = pl.BlockSpec(memory_space=pltpu.VMEM)
    dma = pltpu.SemaphoreType.DMA
    blocks = pl.pallas_call(
        functools.partial(kernel, dims),
        out_shape=jax.ShapeDtypeStruct((group, 2, chunk, WIDTH), bf16),
        in_specs=[
            pl.BlockSpec(memory_space=pltpu.SMEM),
            vmem,
            pl.BlockSpec(memory_space=pl.ANY),
            vmem,
            vmem,
        ],
        out_specs=pl.BlockSpec(memory_space=pl.ANY),
        scratch_shapes=[
            pltpu.VMEM((WIDTH // TILE, WIDTH, TILE), bf16),
            pltpu.VMEM(branch_one.shape, bf16),
            pltpu.VMEM((group, WIDTH, 2 * LANE), bf16),
            pltpu.VMEM((2, WIDTH, WIDTH), bf16),
            pltpu.VMEM((TILES, 2, WIDTH, TILE), bf16),
            pltpu.VMEM((nx * ny, nz, 2, ROWS // nx, LANE), bf16),
            pltpu.VMEM((nx * ny, nz, 2, ROWS // nx, LANE), bf16),
            pltpu.VMEM((nx * ny, nz, 2, ROWS // nx, LANE), bf16),
            pltpu.VMEM((2, group, chunk, WIDTH), bf16),
            pltpu.VMEM((2, group, chunk, WIDTH), bf16),
            pltpu.VMEM((group, 2, chunk, WIDTH), bf16),
            dma((2,)),
            dma((2, nz)),
            dma((3 + 2 * nz,)),
            dma((GROUPS, 4)),
            dma((3,)),
            dma((5,)),
        ],
        compiler_params=pltpu.CompilerParams(
            collective_id=0, has_side_effects=True, vmem_limit_bytes=VMEM_LIMIT
        ),
        cost_estimate=pl.CostEstimate(
            flops=24 * ROWS * WIDTH * WIDTH, bytes_accessed=16 * WIDTH * WIDTH, transcendentals=0
        ),
    )(slice_values, stem.reshape(2, ROWS, WIDTH), branch_one, branch_two, branch_three)
    return blocks.transpose(1, 2, 0, 3).reshape(stem.shape)


def solution(mesh):
    dims = (mesh.shape["gx"], mesh.shape["gy"], mesh.shape["gz"])
    group_one, group_two = dims[0] * dims[1], dims[1] * dims[2]
    fused = group_one == group_two == WIDTH // LANE and dims == (4, 2, 4)
    return jax.shard_map(
        functools.partial(fused_body, dims) if fused else body,
        mesh=mesh,
        in_specs=(
            P(None, "gx", "gy", "gz", None, None),
            P(),
            P(None, None, ("gy", "gz"), None),
            P(None, None, "gz", None),
            P(),
        ),
        out_specs=P(None, "gx", "gy", "gz", None, None),
        check_vma=False,
    )
```
